256 devices in a mesh: gx: 16 (over z, core), gy: 8 (over x, y_lo), seq: 2 (over y_hi).
Axes of the slice: x: 4, y: 4 (y_hi: 2, y_lo: 2; y = y_hi * 2 + y_lo), z: 8, core: 2. Of those that a mesh axis runs over, the one named last changes fastest.
Arguments:
- queries: bfloat16 [32, 64, 16, 1024], P('gx', 'gy', 'seq'), may hold values from -6 to 6
- keys: bfloat16 [2048, 1024], P(('gx', 'gy', 'seq')), may hold values from -8 to 8
- values: bfloat16 [2048, 1024], P(('gx', 'gy', 'seq')), may hold values from -6 to 6
- w_out: bfloat16 [1024, 256], replicated, may hold values from -0.1875 to 0.1875
- conv_first: bfloat16 [3, 3, 3, 256, 128], replicated, may hold values from -0.078125 to 0.078125
- conv_second: bfloat16 [3, 3, 3, 128, 128], replicated, may hold values from -0.109375 to 0.109375
Outputs:
- decoded: bfloat16 [64, 128, 32, 128], P('gx', 'gy', 'seq')
The draws below stay inside these ranges and needn't reach their ends.
All inputs are finite; a program needn't handle non-finite values.
Results may differ from the reference program's by a relative error of at most 0.02.
Values may be sent and summed in bfloat16 or wider, within the bound.
No kernel may reach another device: no remote copies, remote signals or barrier semaphores. Data moves between devices by JAX's collectives and lax.ppermute only.
A program may use at most 64 MiB of HBM per device.

```python
import jax
import jax.numpy as jnp
from jax import lax

H = 8
HD = 128
VOXW = 256
CONV_CH = 128
NX = 32
NY = 64
NZ = 16
TOKENS = 2048


def drawn_pair(key):
    base = jax.random.fold_in(key, 4242)
    key_q, key_k = jax.random.split(base, 2)
    width = H * HD
    nvox = NX * NY * NZ
    query_draw = jnp.clip(jax.random.normal(key_q, (nvox, width), jnp.float32), -6.0, 6.0)
    key_draw = jnp.clip(2.0 * jax.random.normal(key_k, (TOKENS, width), jnp.float32), -8.0, 8.0)
    return (query_draw.reshape(NX, NY, NZ, width), key_draw)


def draw_queries(key, part):
    return drawn_pair(key)[0].astype(jnp.bfloat16)


def draw_keys(key, part):
    return drawn_pair(key)[1].astype(jnp.bfloat16)


def level_of(rng, shape, cuts, low, largest):
    def one(axis_at, shards_of):
        heights = jax.random.uniform(jax.random.fold_in(jax.random.fold_in(rng, 6), axis_at), (shards_of,), jnp.float32, low / len(cuts), largest / len(cuts))
        return jnp.repeat(jnp.exp(heights), shape[axis_at] // shards_of).reshape((-1,) + (1,) * (len(shape) - axis_at - 1))

    loudness = one(*cuts[0])
    for cut in cuts[1:]:
        loudness = loudness * one(*cut)
    return loudness


def scatter_about(own_key, dims, scale, bound, pieces=(), dtype=jnp.bfloat16):
    entries = jax.random.normal(own_key, dims, jnp.float32) * scale
    if len(pieces) > 0:
        entries = level_of(own_key, dims, pieces, -0.22, 0.18) * entries
    return jnp.clip(entries, min=-bound, max=bound).astype(dtype)


def setup_inputs(seed: int = 0) -> dict:
    key_of = jax.random.split(jax.random.key(seed), 7)
    queries = draw_queries(jax.random.fold_in(key_of[6], 71), 0)
    keys = draw_keys(jax.random.fold_in(key_of[6], 71), 0)
    values = scatter_about(key_of[2], (TOKENS, H * HD), 1.0, 6.0, ((0, 256),))
    w_out = scatter_about(key_of[3], (H * HD, VOXW), (H * HD) ** -0.5, 0.1875)
    conv_first = scatter_about(key_of[4], (3, 3, 3, VOXW, CONV_CH), (27 * VOXW) ** -0.5, 0.078125)
    conv_second = scatter_about(key_of[5], (3, 3, 3, CONV_CH, CONV_CH), (27 * CONV_CH) ** -0.5, 0.109375)
    return dict(queries=queries, keys=keys, values=values, w_out=w_out, conv_first=conv_first, conv_second=conv_second)


def conv_layer(padded, weight, size_x, size_y, size_z):
    cin = weight.shape[3]
    cout = weight.shape[4]
    total = jnp.zeros((size_x * size_y * size_z, cout), jnp.float32)
    for a in range(3):
        for b in range(3):
            stacked = jnp.concatenate([padded[a:a + size_x, b:b + size_y, c:c + size_z] for c in range(3)], axis=-1)
            stacked = stacked.reshape(-1, 3 * cin)
            total = total + jnp.dot(stacked, weight[a, b].reshape(3 * cin, cout), preferred_element_type=jnp.float32)
    return total.reshape(size_x, size_y, size_z, cout)

def upsample(field):
    return jnp.repeat(jnp.repeat(jnp.repeat(field, 2, axis=0), 2, axis=1), 2, axis=2)

def reference(queries, keys, values, w_out, conv_first, conv_second):
    nvox = NX * NY * NZ
    scale = HD ** (-0.5)
    query_heads = queries.reshape(nvox, H, HD).transpose(1, 0, 2)
    key_heads = keys.reshape(TOKENS, H, HD).transpose(1, 0, 2)
    value_heads = values.reshape(TOKENS, H, HD).transpose(1, 0, 2)

    def one_head(operands):
        qh, kh, vh = operands
        scores = jnp.dot(qh, kh.T, preferred_element_type=jnp.float32) * scale
        top = lax.optimization_barrier(jnp.max(scores, axis=1, keepdims=True))
        weights = jnp.exp(scores - top).astype(jnp.bfloat16)
        total = lax.optimization_barrier(jnp.sum(weights.astype(jnp.float32), axis=1, keepdims=True))
        summed = jnp.dot(weights, vh, preferred_element_type=jnp.float32)
        return (summed / total).astype(jnp.bfloat16)
    attended = lax.map(one_head, (query_heads, key_heads, value_heads))
    attended = attended.transpose(1, 0, 2).reshape(nvox, H * HD)
    projected = jnp.dot(attended, w_out, preferred_element_type=jnp.float32)
    normed = projected * lax.rsqrt(lax.optimization_barrier(jnp.mean(projected * projected, axis=-1, keepdims=True)) + 1e-06)
    normed = normed.astype(jnp.bfloat16).reshape(NX, NY, NZ, VOXW)
    padded = jnp.pad(normed, ((1, 1), (1, 1), (1, 1), (0, 0)))
    first = conv_layer(padded, conv_first, NX, NY, NZ)
    hidden = jax.nn.silu(first).astype(jnp.bfloat16)
    upsampled = upsample(hidden)
    padded_up = jnp.pad(upsampled, ((1, 1), (1, 1), (1, 1), (0, 0)))
    second = conv_layer(padded_up, conv_second, 2 * NX, 2 * NY, 2 * NZ)
    return second.astype(jnp.bfloat16)
```

```python
import jax
import jax.numpy as jnp
import numpy as np
from jax import lax
from jax.experimental import pallas as pl
from jax.experimental.pallas import tpu as pltpu
from jax.sharding import Mesh, PartitionSpec as P

H = 8
HD = 128
BF = jnp.bfloat16
F32 = jnp.float32
VM = pl.BlockSpec(memory_space=pltpu.VMEM)
LOG2E = 1.4426950408889634


def call(kernel, shape, dtype, count, flops, scratch=()):
    return pl.pallas_call(
        kernel,
        out_shape=jax.ShapeDtypeStruct(shape, dtype),
        in_specs=[VM] * count,
        out_specs=VM,
        scratch_shapes=list(scratch),
        compiler_params=pltpu.CompilerParams(vmem_limit_bytes=48 * 1024 * 1024),
        cost_estimate=pl.CostEstimate(flops=flops, bytes_accessed=1000000, transcendentals=0),
    )


def pack_kernel(q_ref, k_ref, v_ref, out_ref):
    for h in range(H):
        cols = slice(h * HD, (h + 1) * HD)
        pair = jnp.concatenate([k_ref[:, cols].astype(F32), v_ref[:, cols].astype(F32)], axis=0).astype(BF)
        for s in range(2):
            out_ref[2 * h + s, 0:64] = q_ref[s, :, cols]
            out_ref[2 * h + s, 64:80] = pair


def attention_kernel(q_ref, own_ref, other_ref, out_ref):
    keys = jnp.concatenate([own_ref[:, 0:128].reshape(1024, HD), other_ref[:, 0:128].reshape(1024, HD)], axis=0)
    vals = jnp.concatenate([own_ref[:, 128:256].reshape(1024, HD), other_ref[:, 128:256].reshape(1024, HD)], axis=0)
    vals = jnp.concatenate([vals, jnp.ones((2048, HD), BF)], axis=1)
    edge = jnp.zeros((32, HD), BF)
    for s in range(2):
        out_ref[s, 0:32] = edge
        out_ref[14 + s, 160:192] = edge
    for g in range(8):
        q = jnp.concatenate([q_ref[2 * g, 0:64], q_ref[2 * g + 1, 0:64]], axis=0)
        scores = lax.dot_general(q, keys, (((1,), (1,)), ((), ())), preferred_element_type=F32)
        top = jnp.max(scores, axis=1, keepdims=True)
        weights = jnp.exp2((scores - top) * (HD**-0.5 * LOG2E)).astype(BF)
        both = jnp.dot(weights, vals, preferred_element_type=F32)
        done = (both[:, 0:HD] / both[:, HD : 2 * HD]).reshape(2, 8, 8, HD)
        done = jnp.concatenate([done[0], done[1]], axis=1).reshape(128, HD).astype(BF)
        for s in range(2):
            out_ref[2 * g + s, 32:160] = done
            if g < 7:
                out_ref[2 * g + 2 + s, 0:32] = done[96:128]
            if g > 0:
                out_ref[2 * g - 2 + s, 160:192] = done[0:32]


def project_kernel(a_ref, w_ref, out_ref):
    for s in range(2):
        rows = jnp.concatenate([a_ref[2 * h + s] for h in range(H)], axis=1)
        projected = jnp.dot(rows, w_ref[...], preferred_element_type=F32)
        scale = lax.rsqrt(jnp.mean(projected * projected, axis=1, keepdims=True) + 1e-06)
        out_ref[s] = (projected * scale).astype(BF)


def merge_kernel(w_ref, out_ref):
    def both(parts):
        return ((parts[0], parts[1] + parts[2]), (parts[0] + parts[1], parts[2]))

    taps = [[[w_ref[9 * a + 3 * b + c].astype(F32) for c in range(3)] for b in range(3)] for a in range(3)]
    on_z = [[[m for p in both(taps[a][b]) for m in p] for b in range(3)] for a in range(3)]
    for n in range(4):
        on_y = [both([on_z[a][b][n] for b in range(3)]) for a in range(3)]
        for py in range(2):
            for b in range(2):
                on_x = both([on_y[a][py][b] for a in range(3)])
                for px in range(2):
                    for a in range(2):
                        rows = (2 * a + b) * 128
                        out_ref[2 * px + py, rows : rows + 128, n * 128 : (n + 1) * 128] = on_x[px][a].astype(BF)


def shifted(x, by):
    return pltpu.roll(x, by % x.shape[0], 0)


def conv_kernel(where_ref, own_ref, left_ref, right_ref, w1_ref, w2_ref, out_ref, field):
    gx, gy, seq = where_ref[0], where_ref[1], where_ref[2]
    slabs = [left_ref[0], left_ref[1], own_ref[0], own_ref[1], right_ref[0], right_ref[1]]
    row = lax.broadcasted_iota(jnp.int32, (160, 128), 0)
    at_z = row % 16
    at_y = gy * 8 - 1 + row // 16
    inside = (at_y >= 0) & (at_y < 64)
    hidden = []
    for x in range(4):
        total = jnp.zeros((160, 384), F32)
        for a in range(3):
            for b in range(3):
                t = 9 * a + 3 * b
                weight = jnp.concatenate([w1_ref[t], w1_ref[t + 1], w1_ref[t + 2]], axis=1)
                total = total + jnp.dot(slabs[x + a][16 * b : 16 * b + 160], weight, preferred_element_type=F32)
        first = (
            jnp.where(at_z > 0, shifted(total[:, 0:128], 1), 0.0)
            + total[:, 128:256]
            + jnp.where(at_z < 15, shifted(total[:, 256:384], -1), 0.0)
        )
        value = first / (1.0 + jnp.exp(-first))
        at_x = gx * 2 - 1 + x
        value = jnp.where(inside & (at_x >= 0) & (at_x < 32), value, 0.0)
        low = jnp.where(at_z > 0, shifted(value, 1), 0.0)
        high = jnp.where(at_z < 9, shifted(value, -7), 0.0)
        hidden.append(jnp.where(seq == 0, low, high).astype(BF))
    for px in range(2):
        for py in range(2):
            rows = jnp.concatenate(
                [
                    jnp.concatenate(
                        [
                            hidden[i + px + a][16 * (py + b) : 16 * (py + b) + 128]
                            for a in range(2)
                            for b in range(2)
                        ],
                        axis=1,
                    )
                    for i in range(2)
                ],
                axis=0,
            )
            parts = jnp.dot(rows, w2_ref[2 * px + py], preferred_element_type=F32)
            even = parts[:, 0:128] + shifted(parts[:, 128:256], -1)
            odd = shifted(parts[:, 256:384], -1) + shifted(parts[:, 384:512], -2)
            for pz, part in ((0, even), (1, odd)):
                part = part.reshape(2, 8, 16, 128)
                for i in range(2):
                    for j in range(8):
                        field[2 * i + px, 2 * j + py, pl.ds(pz, 8, stride=2), :] = part[i, j, 0:8]
    out_ref[...] = field[...].astype(BF)


def body(queries, keys, values, w_out, conv_first, conv_second):
    plane = ("gy", "seq")
    sent = call(pack_kernel, (16, 80, HD), BF, 3, 1000000)(queries.reshape(2, 64, H * HD), keys, values)
    got = lax.all_to_all(sent, plane, 0, 0, tiled=True)
    pair = got[:, 64:80].reshape(16, 2, 8, HD).transpose(1, 0, 2, 3).reshape(1, 256, HD)
    own = lax.all_to_all(jnp.broadcast_to(pair, (8, 256, HD)), "z", 0, 0, tiled=True)
    other = lax.ppermute(own, "core", [(0, 1), (1, 0)])
    attended = call(attention_kernel, (16, 192, HD), BF, 3, 2 * 10**9)(got, own, other)
    back = lax.all_to_all(attended, plane, 0, 0, tiled=True)
    normed = call(project_kernel, (2, 192, 256), BF, 2, 2 * 10**8)(back, w_out)
    left = lax.ppermute(normed, ("z", "core"), [(i, i + 1) for i in range(15)])
    right = lax.ppermute(normed, ("z", "core"), [(i + 1, i) for i in range(15)])
    merged = call(merge_kernel, (4, 512, 512), BF, 1, 10**9)(conv_second.reshape(27, 128, 128))
    place = jnp.stack([lax.axis_index(("z", "core")), lax.axis_index("gy"), lax.axis_index("seq")]).astype(jnp.int32)
    return pl.pallas_call(
        conv_kernel,
        out_shape=jax.ShapeDtypeStruct((4, 16, 16, 128), BF),
        in_specs=[pl.BlockSpec(memory_space=pltpu.SMEM)] + [VM] * 5,
        out_specs=VM,
        scratch_shapes=[pltpu.VMEM((4, 16, 16, 128), F32)],
        compiler_params=pltpu.CompilerParams(vmem_limit_bytes=48 * 1024 * 1024),
        cost_estimate=pl.CostEstimate(flops=2 * 10**9, bytes_accessed=3000000, transcendentals=0),
    )(place, normed, left, right, conv_first.reshape(27, 256, 128), merged)


def solution(mesh):
    cut = Mesh(mesh.devices.reshape(8, 2, 8, 2), ("z", "core", "gy", "seq"))
    tokens = P(("z", "core", "gy", "seq"), None)
    voxels = P(("z", "core"), "gy", "seq", None)
    return jax.shard_map(
        body, mesh=cut, in_specs=(voxels, tokens, tokens, P(), P(), P()), out_specs=voxels, check_vma=False
    )
```

```python
import jax
import jax.numpy as jnp
from jax import lax
from jax.experimental import pallas as pl
from jax.experimental.pallas import tpu as pltpu
from jax.sharding import Mesh, PartitionSpec as P

H = 8
HD = 128
BF = jnp.bfloat16
F32 = jnp.float32
VM = pl.BlockSpec(memory_space=pltpu.VMEM)
SM = pl.BlockSpec(memory_space=pltpu.SMEM)
HB = pl.BlockSpec(memory_space=pltpu.HBM)
LOG2E = 1.4426950408889634


def call(kernel, shape, dtype, in_specs, scratch=()):
    return pl.pallas_call(
        kernel,
        out_shape=jax.ShapeDtypeStruct(shape, dtype),
        in_specs=in_specs,
        out_specs=VM,
        scratch_shapes=list(scratch),
        compiler_params=pltpu.CompilerParams(vmem_limit_bytes=48 * 1024 * 1024),
        cost_estimate=pl.CostEstimate(flops=10**9, bytes_accessed=1000000, transcendentals=0),
    )


def pack_kernel(q_hbm, k_hbm, v_hbm, out_ref, q_ref, k_ref, v_ref, sems):
    copies = [
        pltpu.make_async_copy(src, dst, sems.at[i])
        for i, (src, dst) in enumerate(((q_hbm, q_ref), (k_hbm, k_ref), (v_hbm, v_ref)))
    ]
    for copy in copies:
        copy.start()
    for copy in copies:
        copy.wait()
    for h in range(H):
        cols = slice(h * HD, (h + 1) * HD)
        pair = jnp.concatenate([k_ref[:, cols].astype(F32), v_ref[:, cols].astype(F32)], axis=0).astype(BF)
        rows = [q_ref[x, :, cols].astype(F32).reshape(8, 8, HD) for x in range(2)]
        rows = jnp.concatenate(rows, axis=1).reshape(128, HD).astype(BF)
        for s in range(2):
            out_ref[2 * h + s, 0:128] = rows
            out_ref[2 * h + s, 128:144] = pair


def attention_kernel(where_ref, q_ref, own_ref, other_ref, out_ref):
    seq = where_ref[2]
    keys = jnp.concatenate([own_ref[:, 0:128].reshape(1024, HD), other_ref[:, 0:128].reshape(1024, HD)], axis=0)
    vals = jnp.concatenate([own_ref[:, 128:256].reshape(1024, HD), other_ref[:, 128:256].reshape(1024, HD)], axis=0)
    vals = jnp.concatenate([vals, jnp.ones((2048, HD), BF)], axis=1)

    def attend(q):
        scores = lax.dot_general(q, keys, (((1,), (1,)), ((), ())), preferred_element_type=F32)
        top = jnp.max(scores, axis=1, keepdims=True)
        weights = jnp.exp2((scores - top) * (HD**-0.5 * LOG2E)).astype(BF)
        both = jnp.dot(weights, vals, preferred_element_type=F32)
        return both[:, 0:HD] / both[:, HD : 2 * HD]

    edge = jnp.zeros((32, HD), BF)
    out_ref[0, 0:32] = edge
    out_ref[7, 160:192] = edge
    for g in range(0, 8, 2):
        pair = attend(jnp.concatenate([q_ref[2 * g + seq, 0:128], q_ref[2 * g + 2 + seq, 0:128]], axis=0)).astype(BF)
        for n, done in ((g, pair[0:128]), (g + 1, pair[128:256])):
            out_ref[n, 32:160] = done
            if n < 7:
                out_ref[n + 1, 0:32] = done[96:128]
            if n > 0:
                out_ref[n - 1, 160:192] = done[0:32]
    row = lax.broadcasted_iota(jnp.int32, (32, 128), 0)
    col = lax.broadcasted_iota(jnp.int32, (32, 128), 1)
    pick = (col == (row // 2) * 8 + row % 2 + 6 * seq).astype(F32).astype(BF)
    near = [jnp.dot(pick, q_ref[2 * g + 1 - seq, 0:128], preferred_element_type=F32).astype(BF) for g in range(8)]
    done = attend(jnp.concatenate(near, axis=0))
    none = jnp.zeros((8, HD), F32)
    done = jnp.concatenate([none, done, none], axis=0)
    for g in range(8):
        out_ref[g, 192:240] = done[32 * g : 32 * g + 48].astype(BF)


def project_kernel(where_ref, a_ref, w_ref, out_ref):
    seq = where_ref[2]
    rows = jnp.concatenate([a_ref[h] for h in range(H)], axis=1)
    projected = jnp.dot(rows, w_ref[...], preferred_element_type=F32)
    scale = lax.rsqrt(jnp.mean(projected * projected, axis=1, keepdims=True) + 1e-06)
    normed = (projected * scale).astype(BF)
    row = lax.broadcasted_iota(jnp.int32, (384, 1), 0)
    x = (row >= 192).astype(jnp.int32)
    y = (row - 192 * x) // 16
    z = row % 16
    near = z - jnp.where(seq == 0, 10, 0)
    source = jnp.where((near >= 0) & (near < 2), 192 + y * 4 + x * 2 + near, -1)
    source = jnp.where((z >= 2) & (z < 10), y * 16 + x * 8 + z - 2, source)
    place = (lax.broadcasted_iota(jnp.int32, (384, 240), 1) == source).astype(F32).astype(BF)
    out_ref[...] = jnp.dot(place, normed, preferred_element_type=F32).astype(BF).reshape(2, 192, 256)


def merge_kernel(w_ref, out_ref):
    def both(parts):
        return ((parts[0], parts[1] + parts[2]), (parts[0] + parts[1], parts[2]))

    taps = [[[w_ref[9 * a + 3 * b + c].astype(F32) for c in range(3)] for b in range(3)] for a in range(3)]
    on_z = [[[m for p in both(taps[a][b]) for m in p] for b in range(3)] for a in range(3)]
    for n in range(4):
        on_y = [both([on_z[a][b][n] for b in range(3)]) for a in range(3)]
        for py in range(2):
            for b in range(2):
                on_x = both([on_y[a][py][b] for a in range(3)])
                for px in range(2):
                    for a in range(2):
                        rows = (2 * a + b) * 128
                        out_ref[2 * px + py, rows : rows + 128, n * 128 : (n + 1) * 128] = on_x[px][a].astype(BF)


def shifted(x, by):
    return pltpu.roll(x, by % x.shape[0], 0)


def conv_kernel(where_ref, own_ref, near_ref, far_ref, w1_ref, w2_ref, out_ref, field):
    gx, gy, seq = where_ref[0], where_ref[1], where_ref[2]
    first_core = gx % 2 == 0
    none = jnp.zeros((192, 256), BF)
    slabs = [own_ref[0], own_ref[1]]
    left = [jnp.where(gx == 0, none, jnp.where(first_core, far_ref[x], near_ref[x])) for x in range(2)]
    right = [jnp.where(gx == 15, none, jnp.where(first_core, near_ref[x], far_ref[x])) for x in range(2)]
    slabs = left + slabs + right
    row = lax.broadcasted_iota(jnp.int32, (160, 128), 0)
    at_z = seq * 8 - 1 + row % 16
    at_y = gy * 8 - 1 + row // 16
    inside = (at_y >= 0) & (at_y < 64) & (at_z >= 0) & (at_z < 16)
    hidden = []
    for x in range(4):
        total = jnp.zeros((160, 384), F32)
        for a in range(3):
            for b in range(3):
                t = 9 * a + 3 * b
                weight = jnp.concatenate([w1_ref[t], w1_ref[t + 1], w1_ref[t + 2]], axis=1)
                total = total + jnp.dot(slabs[x + a][16 * b : 16 * b + 160], weight, preferred_element_type=F32)
        first = total[:, 0:128] + shifted(total[:, 128:256], -1) + shifted(total[:, 256:384], -2)
        value = first / (1.0 + jnp.exp(-first))
        at_x = gx * 2 - 1 + x
        hidden.append(jnp.where(inside & (at_x >= 0) & (at_x < 32), value, 0.0).astype(BF))
    for px in range(2):
        for py in range(2):
            rows = jnp.concatenate(
                [
                    jnp.concatenate(
                        [
                            hidden[i + px + a][16 * (py + b) : 16 * (py + b) + 128]
                            for a in range(2)
                            for b in range(2)
                        ],
                        axis=1,
                    )
                    for i in range(2)
                ],
                axis=0,
            )
            parts = jnp.dot(rows, w2_ref[2 * px + py], preferred_element_type=F32)
            even = parts[:, 0:128] + shifted(parts[:, 128:256], -1)
            odd = shifted(parts[:, 256:384], -1) + shifted(parts[:, 384:512], -2)
            for pz, part in ((0, even), (1, odd)):
                part = part.reshape(2, 8, 16, 128)
                for i in range(2):
                    for j in range(8):
                        field[2 * i + px, 2 * j + py, pl.ds(pz, 8, stride=2), :] = part[i, j, 0:8]
    out_ref[...] = field[...].astype(BF)


def body(queries, keys, values, w_out, conv_first, conv_second):
    z, core, gy, seq = (lax.axis_index(name) for name in ("z", "core", "gy", "seq"))
    place = jnp.stack([2 * z + core, gy, seq]).astype(jnp.int32)
    sent = call(
        pack_kernel,
        (16, 144, HD),
        BF,
        [HB] * 3,
        [
            pltpu.VMEM((2, 64, H * HD), BF),
            pltpu.VMEM((8, H * HD), BF),
            pltpu.VMEM((8, H * HD), BF),
            pltpu.SemaphoreType.DMA((3,)),
        ],
    )(queries.reshape(2, 64, H * HD), keys, values)
    got = lax.all_to_all(sent, ("gy", "seq"), 0, 0, tiled=True)
    pair = got[:, 128:144].reshape(16, 2, 8, HD).transpose(1, 0, 2, 3).reshape(1, 256, HD)
    own = lax.all_to_all(jnp.broadcast_to(pair, (8, 256, HD)), "z", 0, 0, tiled=True)
    other = lax.ppermute(own, "core", [(0, 1), (1, 0)])
    attended = call(attention_kernel, (8, 240, HD), BF, [SM] + [VM] * 3)(place, got, own, other)
    back = lax.all_to_all(attended, "gy", 0, 0, tiled=True)
    normed = call(project_kernel, (2, 192, 256), BF, [SM] + [VM] * 2)(place, back, w_out)
    far = lax.ppermute(normed, ("z", "core"), [(i, (i - 1 + 2 * (i % 2)) % 16) for i in range(16)])
    near = lax.ppermute(normed, "core", [(0, 1), (1, 0)])
    merged = call(merge_kernel, (4, 512, 512), BF, [VM])(conv_second.reshape(27, 128, 128))
    return call(conv_kernel, (4, 16, 16, 128), BF, [SM] + [VM] * 5, [pltpu.VMEM((4, 16, 16, 128), F32)])(
        place, normed, near, far, conv_first.reshape(27, 256, 128), merged
    )


def solution(mesh):
    cut = Mesh(mesh.devices.reshape(8, 2, 8, 2), ("z", "core", "gy", "seq"))
    tokens = P(("z", "core", "gy", "seq"), None)
    voxels = P(("z", "core"), "gy", "seq", None)
    return jax.shard_map(
        body, mesh=cut, in_specs=(voxels, tokens, tokens, P(), P(), P()), out_specs=voxels, check_vma=False
    )
```

```python
import jax
import jax.numpy as jnp
from jax import lax
from jax.experimental import pallas as pl
from jax.experimental.pallas import tpu as pltpu
from jax.sharding import Mesh, PartitionSpec as P

H = 8
HD = 128
BF = jnp.bfloat16
F32 = jnp.float32
VM = pl.BlockSpec(memory_space=pltpu.VMEM)
SM = pl.BlockSpec(memory_space=pltpu.SMEM)
HB = pl.BlockSpec(memory_space=pltpu.HBM)
SCALE = HD**-0.5 * 1.4426950408889634


def call(kernel, shapes, dtypes, in_specs, scratch=(), room=48):
    outs = [jax.ShapeDtypeStruct(shape, dtype) for shape, dtype in zip(shapes, dtypes)]
    one = len(outs) == 1
    return pl.pallas_call(
        kernel,
        out_shape=outs[0] if one else outs,
        in_specs=in_specs,
        out_specs=VM if one else [VM] * len(outs),
        scratch_shapes=list(scratch),
        compiler_params=pltpu.CompilerParams(vmem_limit_bytes=room * 1024 * 1024),
        cost_estimate=pl.CostEstimate(flops=10**9, bytes_accessed=1000000, transcendentals=0),
    )


def pack_kernel(q_hbm, k_hbm, v_hbm, out_ref, q_ref, k_ref, v_ref, sems):
    copies = [
        pltpu.make_async_copy(src, dst, sems.at[i])
        for i, (src, dst) in enumerate(((q_hbm, q_ref), (k_hbm, k_ref), (v_hbm, v_ref)))
    ]
    for copy in copies:
        copy.start()
    for copy in copies:
        copy.wait()
    for h in range(H):
        cols = slice(h * HD, (h + 1) * HD)
        pair = jnp.concatenate([k_ref[:, cols].astype(F32), v_ref[:, cols].astype(F32)], axis=0).astype(BF)
        rows = [q_ref[x, :, cols].astype(F32).reshape(8, 8, HD) for x in range(2)]
        rows = jnp.concatenate(rows, axis=1).reshape(128, HD).astype(BF)
        for s in range(2):
            out_ref[2 * h + s, 0:128] = rows
            out_ref[2 * h + s, 128:144] = pair


def halves(ref):
    keys = ref[:, 0:128].reshape(1024, HD)
    return keys, jnp.concatenate([ref[:, 128:256].reshape(1024, HD), jnp.ones((1024, HD), BF)], axis=1)


def scores_of(q, keys):
    scores = lax.dot_general(q, keys, (((1,), (1,)), ((), ())), preferred_element_type=F32)
    return scores, jnp.max(scores, axis=1, keepdims=True)


def first_half_kernel(where_ref, q_ref, kv_ref, q_out, sum_out, top_out):
    seq = where_ref[2]
    keys, vals = halves(kv_ref)
    row = lax.broadcasted_iota(jnp.int32, (32, 128), 0)
    col = lax.broadcasted_iota(jnp.int32, (32, 128), 1)
    pick = (col == (row // 2) * 8 + row % 2 + 6 * seq).astype(F32).astype(BF)
    near = [jnp.dot(pick, q_ref[2 * g + 1 - seq, 0:128], preferred_element_type=F32).astype(BF) for g in range(8)]
    for n in range(10):
        rows = slice(128 * n, 128 * n + 128)
        q = q_ref[2 * n + seq, 0:128] if n < 8 else jnp.concatenate(near[4 * n - 32 : 4 * n - 28], axis=0)
        scores, top = scores_of(q, keys)
        weights = jnp.exp2((scores - top) * SCALE).astype(BF)
        q_out[rows] = q
        sum_out[rows] = jnp.dot(weights, vals, preferred_element_type=F32)
        top_out[rows] = jnp.broadcast_to(top, (128, HD))


def second_half_kernel(q_ref, kv_ref, sum_ref, top_ref, out_ref):
    keys, vals = halves(kv_ref)
    edge = jnp.zeros((32, HD), BF)
    out_ref[0, 0:32] = edge
    out_ref[7, 160:192] = edge
    near = []
    for n in range(10):
        rows = slice(128 * n, 128 * n + 128)
        scores, top = scores_of(q_ref[rows], keys)
        before = top_ref[rows, 0:1]
        top = jnp.maximum(top, before)
        weights = jnp.exp2((scores - top) * SCALE).astype(BF)
        kept = jnp.exp2((before - top) * SCALE)
        both = sum_ref[rows] * kept + jnp.dot(weights, vals, preferred_element_type=F32)
        done = both[:, 0:HD] / both[:, HD : 2 * HD]
        if n >= 8:
            near.append(done)
            continue
        done = done.astype(BF)
        out_ref[n, 32:160] = done
        if n < 7:
            out_ref[n + 1, 0:32] = done[96:128]
        if n > 0:
            out_ref[n - 1, 160:192] = done[0:32]
    none = jnp.zeros((8, HD), F32)
    near = jnp.concatenate([none] + near + [none], axis=0)
    for g in range(8):
        out_ref[g, 192:240] = near[32 * g : 32 * g + 48].astype(BF)


def project_kernel(where_ref, a_ref, w_ref, out_ref):
    seq = where_ref[2]
    rows = jnp.concatenate([a_ref[h] for h in range(H)], axis=1)
    projected = jnp.dot(rows, w_ref[...], preferred_element_type=F32)
    scale = lax.rsqrt(jnp.mean(projected * projected, axis=1, keepdims=True) + 1e-06)
    normed = projected * scale
    half = normed[0:192].reshape(12, 2, 8, 256)
    near = normed[192:240].reshape(6, 8, 256)
    row = lax.broadcasted_iota(jnp.int32, (12, 8, 256), 1)
    for x in range(2):
        middle = pltpu.roll(half[:, x], 2, 1)
        ends = [pltpu.roll(near, (8 - 4 * odd - 2 * x) % 8, 1) if odd + x else near for odd in range(2)]
        ends = jnp.stack(ends, axis=1).reshape(12, 8, 256)
        upper = jnp.where(row < 2, jnp.where(seq == 1, ends, 0.0), middle)
        lower = jnp.where((row < 4) & (seq == 0), pltpu.roll(ends, 2, 1), 0.0)
        lower = jnp.where(row < 2, middle, lower)
        out_ref[x] = jnp.concatenate([upper, lower], axis=1).reshape(192, 256).astype(BF)


def merge_kernel(w_ref, out_ref):
    def both(parts):
        return ((parts[0], parts[1] + parts[2]), (parts[0] + parts[1], parts[2]))

    taps = [[[w_ref[9 * a + 3 * b + c].astype(F32) for c in range(3)] for b in range(3)] for a in range(3)]
    on_z = [[[m for p in both(taps[a][b]) for m in p] for b in range(3)] for a in range(3)]
    for n in range(4):
        on_y = [both([on_z[a][b][n] for b in range(3)]) for a in range(3)]
        for py in range(2):
            for b in range(2):
                on_x = both([on_y[a][py][b] for a in range(3)])
                for px in range(2):
                    for a in range(2):
                        rows = (2 * a + b) * 128
                        out_ref[2 * px + py, rows : rows + 128, n * 128 : (n + 1) * 128] = on_x[px][a].astype(BF)


def shifted(x, by):
    return pltpu.roll(x, by % x.shape[0], 0)


def taps(w1_ref, a, b):
    t = 9 * a + 3 * b
    return jnp.concatenate([w1_ref[t], w1_ref[t + 1], w1_ref[t + 2]], axis=1)


def own_conv_kernel(own_ref, w1_ref, out_ref):
    for x in range(4):
        total = jnp.zeros((160, 384), F32)
        for a in range(3):
            if 2 <= x + a < 4:
                for b in range(3):
                    part = own_ref[x + a - 2, 16 * b : 16 * b + 160]
                    total = total + jnp.dot(part, taps(w1_ref, a, b), preferred_element_type=F32)
        out_ref[x] = total


def conv_kernel(where_ref, own_ref, near_ref, far_ref, w1_ref, w2_ref, out_ref, field):
    gx, gy, seq = where_ref[0], where_ref[1], where_ref[2]
    first_core = gx % 2 == 0
    none = jnp.zeros((192, 256), BF)
    left = [jnp.where(gx == 0, none, jnp.where(first_core, far_ref[x], near_ref[x])) for x in range(2)]
    right = [jnp.where(gx == 15, none, jnp.where(first_core, near_ref[x], far_ref[x])) for x in range(2)]
    slabs = left + [None, None] + right
    row = lax.broadcasted_iota(jnp.int32, (160, 128), 0)
    at_z = seq * 8 - 1 + row % 16
    at_y = gy * 8 - 1 + row // 16
    inside = (at_y >= 0) & (at_y < 64) & (at_z >= 0) & (at_z < 16)
    hidden = []
    for x in range(4):
        total = own_ref[x]
        for a in range(3):
            if slabs[x + a] is not None:
                for b in range(3):
                    part = slabs[x + a][16 * b : 16 * b + 160]
                    total = total + jnp.dot(part, taps(w1_ref, a, b), preferred_element_type=F32)
        first = total[:, 0:128] + shifted(total[:, 128:256], -1) + shifted(total[:, 256:384], -2)
        value = first / (1.0 + jnp.exp(-first))
        at_x = gx * 2 - 1 + x
        hidden.append(jnp.where(inside & (at_x >= 0) & (at_x < 32), value, 0.0).astype(BF))
    for px in range(2):
        for py in range(2):
            rows = jnp.concatenate(
                [
                    jnp.concatenate(
                        [
                            hidden[i + px + a][16 * (py + b) : 16 * (py + b) + 128]
                            for a in range(2)
                            for b in range(2)
                        ],
                        axis=1,
                    )
                    for i in range(2)
                ],
                axis=0,
            )
            parts = jnp.dot(rows, w2_ref[2 * px + py], preferred_element_type=F32)
            even = parts[:, 0:128] + shifted(parts[:, 128:256], -1)
            odd = shifted(parts[:, 256:384], -1) + shifted(parts[:, 384:512], -2)
            for pz, part in ((0, even), (1, odd)):
                part = part.reshape(2, 8, 16, 128)
                for i in range(2):
                    for j in range(8):
                        field[2 * i + px, 2 * j + py, pl.ds(pz, 8, stride=2), :] = part[i, j, 0:8]
    out_ref[...] = field[...].astype(BF)


def body(queries, keys, values, w_out, conv_first, conv_second):
    z, core, gy, seq = (lax.axis_index(name) for name in ("z", "core", "gy", "seq"))
    place = jnp.stack([2 * z + core, gy, seq]).astype(jnp.int32)
    sent = call(
        pack_kernel,
        [(16, 144, HD)],
        [BF],
        [HB] * 3,
        [
            pltpu.VMEM((2, 64, H * HD), BF),
            pltpu.VMEM((8, H * HD), BF),
            pltpu.VMEM((8, H * HD), BF),
            pltpu.SemaphoreType.DMA((3,)),
        ],
        room=62,
    )(queries.reshape(2, 64, H * HD), keys, values)
    got = lax.all_to_all(sent, ("gy", "seq"), 0, 0, tiled=True)
    pair = got[:, 128:144].reshape(16, 2, 8, HD).transpose(1, 0, 2, 3).reshape(1, 256, HD)
    own = lax.all_to_all(jnp.broadcast_to(pair, (8, 256, HD)), "z", 0, 0, tiled=True)
    other = lax.ppermute(own, "core", [(0, 1), (1, 0)])
    half = call(first_half_kernel, [(1280, HD), (1280, 2 * HD), (1280, HD)], [BF, F32, F32], [SM, VM, VM])
    q, summed, top = half(place, got, own)
    attended = call(second_half_kernel, [(8, 240, HD)], [BF], [VM] * 4)(q, other, summed, top)
    back = lax.all_to_all(attended, "gy", 0, 0, tiled=True)
    normed = call(project_kernel, [(2, 192, 256)], [BF], [SM, VM, VM])(place, back, w_out)
    far = lax.ppermute(normed, ("z", "core"), [(i, (i - 1 + 2 * (i % 2)) % 16) for i in range(16)])
    near = lax.ppermute(normed, "core", [(0, 1), (1, 0)])
    w1 = conv_first.reshape(27, 256, 128)
    own_part = call(own_conv_kernel, [(4, 160, 384)], [F32], [VM, VM])(normed, w1)
    merged = call(merge_kernel, [(4, 512, 512)], [BF], [VM])(conv_second.reshape(27, 128, 128))
    final = call(conv_kernel, [(4, 16, 16, 128)], [BF], [SM] + [VM] * 5, [pltpu.VMEM((4, 16, 16, 128), F32)])
    return final(place, own_part, near, far, w1, merged)


def solution(mesh):
    cut = Mesh(mesh.devices.reshape(8, 2, 8, 2), ("z", "core", "gy", "seq"))
    tokens = P(("z", "core", "gy", "seq"), None)
    voxels = P(("z", "core"), "gy", "seq", None)
    return jax.shard_map(
        body, mesh=cut, in_specs=(voxels, tokens, tokens, P(), P(), P()), out_specs=voxels, check_vma=False
    )
```

```python
import jax
import jax.numpy as jnp
from jax import lax
from jax.experimental import pallas as pl
from jax.experimental.pallas import tpu as pltpu
from jax.sharding import Mesh, PartitionSpec as P

H = 8
HD = 128
BF = jnp.bfloat16
F32 = jnp.float32
VM = pl.BlockSpec(memory_space=pltpu.VMEM)
SM = pl.BlockSpec(memory_space=pltpu.SMEM)
HB = pl.BlockSpec(memory_space=pltpu.HBM)
SCALE = HD**-0.5 * 1.4426950408889634


def call(kernel, shapes, dtypes, in_specs, scratch=(), out_spec=VM):
    outs = [jax.ShapeDtypeStruct(shape, dtype) for shape, dtype in zip(shapes, dtypes)]
    one = len(outs) == 1
    return pl.pallas_call(
        kernel,
        out_shape=outs[0] if one else outs,
        in_specs=in_specs,
        out_specs=out_spec if one else [VM] * len(outs),
        scratch_shapes=list(scratch),
        compiler_params=pltpu.CompilerParams(vmem_limit_bytes=24 * 1024 * 1024),
        cost_estimate=pl.CostEstimate(flops=10**9, bytes_accessed=1000000, transcendentals=0),
    )


def pack_kernel(q_hbm, k_hbm, v_hbm, out_ref, q_ref, k_ref, v_ref, sems):
    copies = [
        pltpu.make_async_copy(src, dst, sems.at[i])
        for i, (src, dst) in enumerate(((q_hbm, q_ref), (k_hbm, k_ref), (v_hbm, v_ref)))
    ]
    for copy in copies:
        copy.start()
    for copy in copies:
        copy.wait()
    for h in range(H):
        cols = slice(h * HD, (h + 1) * HD)
        pair = jnp.concatenate([k_ref[:, cols].astype(F32), v_ref[:, cols].astype(F32)], axis=0).astype(BF)
        for s in range(2):
            out_ref[2 * h + s, 0:64] = q_ref[0, :, cols]
            out_ref[2 * h + s, 64:128] = q_ref[1, :, cols]
            out_ref[2 * h + s, 128:144] = pair


def halves(ref):
    keys = ref[:, 0:128].reshape(1024, HD)
    return keys, jnp.concatenate([ref[:, 128:256].reshape(1024, HD), jnp.ones((1024, HD), BF)], axis=1)


def scores_of(q, keys):
    scores = lax.dot_general(q, keys, (((1,), (1,)), ((), ())), preferred_element_type=F32)
    return scores, jnp.max(scores, axis=1, keepdims=True)


def first_half_kernel(where_ref, q_ref, kv_ref, q_out, sum_out, top_out):
    seq = where_ref[2]
    keys, vals = halves(kv_ref)
    row = lax.broadcasted_iota(jnp.int32, (32, 128), 0)
    col = lax.broadcasted_iota(jnp.int32, (32, 128), 1)
    pick = (col == (row // 2) % 2 * 64 + (row // 4) * 8 + row % 2 + 6 * seq).astype(F32).astype(BF)
    near = [jnp.dot(pick, q_ref[2 * g + 1 - seq, 0:128], preferred_element_type=F32).astype(BF) for g in range(8)]
    for n in range(10):
        rows = slice(128 * n, 128 * n + 128)
        q = q_ref[2 * n + seq, 0:128] if n < 8 else jnp.concatenate(near[4 * n - 32 : 4 * n - 28], axis=0)
        scores, top = scores_of(q, keys)
        weights = jnp.exp2((scores - top) * SCALE).astype(BF)
        q_out[rows] = q
        sum_out[rows] = jnp.dot(weights, vals, preferred_element_type=F32)
        top_out[rows] = jnp.broadcast_to(top, (128, HD))


def second_half_kernel(q_ref, kv_ref, sum_ref, top_ref, out_ref):
    keys, vals = halves(kv_ref)
    edge = jnp.zeros((32, HD), BF)
    out_ref[0, 0:32] = edge
    out_ref[7, 160:192] = edge
    near = []
    for n in range(10):
        rows = slice(128 * n, 128 * n + 128)
        scores, top = scores_of(q_ref[rows], keys)
        before = top_ref[rows, 0:1]
        top = jnp.maximum(top, before)
        weights = jnp.exp2((scores - top) * SCALE).astype(BF)
        kept = jnp.exp2((before - top) * SCALE)
        both = sum_ref[rows] * kept + jnp.dot(weights, vals, preferred_element_type=F32)
        done = both[:, 0:HD] / both[:, HD : 2 * HD]
        if n >= 8:
            near.append(done)
            continue
        done = done.reshape(2, 8, 8, HD)
        done = jnp.concatenate([done[0], done[1]], axis=1).reshape(128, HD).astype(BF)
        out_ref[n, 32:160] = done
        if n < 7:
            out_ref[n + 1, 0:32] = done[96:128]
        if n > 0:
            out_ref[n - 1, 160:192] = done[0:32]
    none = jnp.zeros((8, HD), F32)
    near = jnp.concatenate([none] + near + [none], axis=0)
    for g in range(8):
        out_ref[g, 192:240] = near[32 * g : 32 * g + 48].astype(BF)


def project_kernel(a_ref, w_ref, out_ref):
    rows = jnp.concatenate([a_ref[h] for h in range(H)], axis=1)
    projected = jnp.dot(rows, w_ref[...], preferred_element_type=F32)
    scale = lax.rsqrt(jnp.mean(projected * projected, axis=1, keepdims=True) + 1e-06)
    out_ref[...] = (projected * scale).astype(BF)


def laid_out(normed, seq):
    half = normed[0:192].astype(F32).reshape(12, 2, 8, 256)
    near = normed[192:240].astype(F32).reshape(6, 8, 256)
    row = lax.broadcasted_iota(jnp.int32, (12, 8, 256), 1)
    slabs = []
    for x in range(2):
        middle = pltpu.roll(half[:, x], 2, 1)
        ends = [pltpu.roll(near, (8 - 4 * odd - 2 * x) % 8, 1) if odd + x else near for odd in range(2)]
        ends = jnp.stack(ends, axis=1).reshape(12, 8, 256)
        upper = jnp.where(row < 2, jnp.where(seq == 1, ends, 0.0), middle)
        lower = jnp.where((row < 4) & (seq == 0), pltpu.roll(ends, 2, 1), 0.0)
        lower = jnp.where(row < 2, middle, lower)
        slabs.append(jnp.concatenate([upper, lower], axis=1).reshape(192, 256).astype(BF))
    return slabs


def merge_kernel(w_ref, out_ref):
    def both(parts):
        return ((parts[0], parts[1] + parts[2]), (parts[0] + parts[1], parts[2]))

    taps = [[[w_ref[9 * a + 3 * b + c].astype(F32) for c in range(3)] for b in range(3)] for a in range(3)]
    on_z = [[[m for p in both(taps[a][b]) for m in p] for b in range(3)] for a in range(3)]
    for n in range(4):
        on_y = [both([on_z[a][b][n] for b in range(3)]) for a in range(3)]
        for py in range(2):
            for b in range(2):
                on_x = both([on_y[a][py][b] for a in range(3)])
                for px in range(2):
                    for a in range(2):
                        rows = (2 * a + b) * 128
                        out_ref[2 * px + py, rows : rows + 128, n * 128 : (n + 1) * 128] = on_x[px][a].astype(BF)


def shifted(x, by):
    return pltpu.roll(x, by % x.shape[0], 0)


def taps(w1_ref, a, b):
    t = 9 * a + 3 * b
    return jnp.concatenate([w1_ref[t], w1_ref[t + 1], w1_ref[t + 2]], axis=1)


def own_conv_kernel(where_ref, own_ref, w1_ref, out_ref):
    slabs = laid_out(own_ref[...], where_ref[2])
    for x in range(4):
        total = jnp.zeros((160, 384), F32)
        for a in range(3):
            if 2 <= x + a < 4:
                for b in range(3):
                    part = slabs[x + a - 2][16 * b : 16 * b + 160]
                    total = total + jnp.dot(part, taps(w1_ref, a, b), preferred_element_type=F32)
        out_ref[x] = total


def side(where_ref, at_left, slabs, own_ref, w1_ref):
    gx, gy, seq = where_ref[0], where_ref[1], where_ref[2]
    row = lax.broadcasted_iota(jnp.int32, (160, 128), 0)
    at_z = seq * 8 - 1 + row % 16
    at_y = gy * 8 - 1 + row // 16
    inside = (at_y >= 0) & (at_y < 64) & (at_z >= 0) & (at_z < 16)
    first_tap = jnp.where(at_left, 0, 1)
    outer = [(slabs[0], first_tap), (slabs[1], first_tap + 1)]
    inner = [(jnp.where(at_left, slabs[1], slabs[0]), jnp.where(at_left, 0, 2))]
    results = []
    for x, terms in ((jnp.where(at_left, 0, 3), outer), (jnp.where(at_left, 1, 2), inner)):
        total = own_ref[x]
        for slab, a in terms:
            for b in range(3):
                total = total + jnp.dot(slab[16 * b : 16 * b + 160], taps(w1_ref, a, b), preferred_element_type=F32)
        first = total[:, 0:128] + shifted(total[:, 128:256], -1) + shifted(total[:, 256:384], -2)
        value = first / (1.0 + jnp.exp(-first))
        at_x = gx * 2 - 1 + x
        results.append((x, jnp.where(inside & (at_x >= 0) & (at_x < 32), value, 0.0).astype(BF)))
    return results


def near_conv_kernel(where_ref, near_ref, own_ref, w1_ref, out_ref):
    at_left = where_ref[0] % 2 == 1
    slabs = laid_out(near_ref[...], where_ref[2])
    for n, (_, rows) in enumerate(side(where_ref, at_left, slabs, own_ref, w1_ref)):
        out_ref[n] = rows


def conv_kernel(where_ref, own_ref, done_ref, far_ref, w1_ref, w2_ref, out_hbm, hidden, field, ready, sems):
    gx = where_ref[0]
    at_left = gx % 2 == 0
    there = jnp.where(at_left, gx > 0, gx < 15)
    slabs = [jnp.where(there, slab, jnp.zeros_like(slab)) for slab in laid_out(far_ref[...], where_ref[2])]
    hidden[jnp.where(at_left, 3, 0)] = done_ref[0]
    hidden[jnp.where(at_left, 2, 1)] = done_ref[1]
    for x, rows in side(where_ref, at_left, slabs, own_ref, w1_ref):
        hidden[x] = rows
    copies = []
    for px in range(2):
        for py in range(2):
            rows = [
                [hidden[i + px + a, 16 * (py + b) : 16 * (py + b) + 128] for a in range(2) for b in range(2)]
                for i in range(2)
            ]
            rows = jnp.concatenate([jnp.concatenate(parts, axis=1) for parts in rows], axis=0)
            parts = jnp.dot(rows, w2_ref[2 * px + py], preferred_element_type=F32)
            even = parts[:, 0:128] + shifted(parts[:, 128:256], -1)
            odd = shifted(parts[:, 256:384], -1) + shifted(parts[:, 384:512], -2)
            for pz, part in ((0, even), (1, odd)):
                part = part.reshape(2, 8, 16, 128)
                for i in range(2):
                    for j in range(8):
                        field[2 * i + px, 2 * j + py, pl.ds(pz, 8, stride=2), :] = part[i, j, 0:8]
        for x in (px, px + 2):
            ready[x] = field[x].astype(BF)
            copies.append(pltpu.make_async_copy(ready.at[x], out_hbm.at[x], sems.at[x]))
            copies[-1].start()
    for copy in copies:
        copy.wait()


def body(queries, keys, values, w_out, conv_first, conv_second):
    z, core, gy, seq = (lax.axis_index(name) for name in ("z", "core", "gy", "seq"))
    place = jnp.stack([2 * z + core, gy, seq]).astype(jnp.int32)
    sent = call(
        pack_kernel,
        [(16, 144, HD)],
        [BF],
        [HB] * 3,
        [
            pltpu.VMEM((2, 64, H * HD), BF),
            pltpu.VMEM((8, H * HD), BF),
            pltpu.VMEM((8, H * HD), BF),
            pltpu.SemaphoreType.DMA((3,)),
        ],
    )(*(pltpu.with_memory_space_constraint(a, pltpu.HBM) for a in (queries.reshape(2, 64, H * HD), keys, values)))
    got = lax.all_to_all(sent, ("gy", "seq"), 0, 0, tiled=True)
    pair = got[:, 128:144].reshape(16, 2, 8, HD).transpose(1, 0, 2, 3).reshape(1, 256, HD)
    own = lax.all_to_all(jnp.broadcast_to(pair, (8, 256, HD)), "z", 0, 0, tiled=True)
    other = lax.ppermute(own, "core", [(0, 1), (1, 0)])
    half = call(first_half_kernel, [(1280, HD), (1280, 2 * HD), (1280, HD)], [BF, F32, F32], [SM, VM, VM])
    q, summed, top = half(place, got, own)
    attended = call(second_half_kernel, [(8, 240, HD)], [BF], [VM] * 4)(q, other, summed, top)
    back = lax.all_to_all(attended, "gy", 0, 0, tiled=True)
    normed = call(project_kernel, [(240, 256)], [BF], [VM, VM])(back, w_out)
    far = lax.ppermute(normed, ("z", "core"), [(i, (i - 1 + 2 * (i % 2)) % 16) for i in range(16)])
    near = lax.ppermute(normed, "core", [(0, 1), (1, 0)])
    w1 = conv_first.reshape(27, 256, 128)
    merged = call(merge_kernel, [(4, 512, 512)], [BF], [VM])(conv_second.reshape(27, 128, 128))
    own_part = call(own_conv_kernel, [(4, 160, 384)], [F32], [SM, VM, VM])(place, normed, w1)
    done = call(near_conv_kernel, [(2, 160, 128)], [BF], [SM] + [VM] * 3)(place, near, own_part, w1)
    scratch = [
        pltpu.VMEM((4, 160, 128), BF),
        pltpu.VMEM((4, 16, 16, 128), F32),
        pltpu.VMEM((4, 16, 16, 128), BF),
        pltpu.SemaphoreType.DMA((4,)),
    ]
    final = call(conv_kernel, [(4, 16, 16, 128)], [BF], [SM] + [VM] * 5, scratch, HB)
    return final(place, own_part, done, far, w1, merged)


def solution(mesh):
    cut = Mesh(mesh.devices.reshape(8, 2, 8, 2), ("z", "core", "gy", "seq"))
    tokens = P(("z", "core", "gy", "seq"), None)
    voxels = P(("z", "core"), "gy", "seq", None)
    return jax.shard_map(
        body, mesh=cut, in_specs=(voxels, tokens, tokens, P(), P(), P()), out_specs=voxels, check_vma=False
    )
```

```python
import jax
import jax.numpy as jnp
from jax import lax
from jax.experimental import pallas as pl
from jax.experimental.pallas import tpu as pltpu
from jax.sharding import Mesh, PartitionSpec as P

H = 8
HD = 128
BF = jnp.bfloat16
F32 = jnp.float32
VM = pl.BlockSpec(memory_space=pltpu.VMEM)
HB = pl.BlockSpec(memory_space=pltpu.HBM)
SCALE = HD**-0.5 * 1.4426950408889634


def call(kernel, shapes, dtypes, in_specs, scratch=(), out_spec=VM):
    outs = [jax.ShapeDtypeStruct(shape, dtype) for shape, dtype in zip(shapes, dtypes)]
    one = len(outs) == 1
    return pl.pallas_call(
        kernel,
        out_shape=outs[0] if one else outs,
        in_specs=in_specs,
        out_specs=out_spec if one else [VM] * len(outs),
        scratch_shapes=list(scratch),
        compiler_params=pltpu.CompilerParams(vmem_limit_bytes=24 * 1024 * 1024),
        cost_estimate=pl.CostEstimate(flops=10**6, bytes_accessed=10000, transcendentals=0),
    )


def pack_kernel(q_hbm, k_hbm, v_hbm, out_ref, q_ref, k_ref, v_ref, sems):
    copies = [
        pltpu.make_async_copy(src, dst, sems.at[i])
        for i, (src, dst) in enumerate(((q_hbm, q_ref), (k_hbm, k_ref), (v_hbm, v_ref)))
    ]
    for copy in copies:
        copy.start()
    for copy in copies:
        copy.wait()
    for h in range(H):
        cols = slice(h * HD, (h + 1) * HD)
        pair = jnp.concatenate([k_ref[:, cols].astype(F32), v_ref[:, cols].astype(F32)], axis=0).astype(BF)
        for s in range(2):
            out_ref[2 * h + s, 0:64] = q_ref[0, :, cols]
            out_ref[2 * h + s, 64:128] = q_ref[1, :, cols]
            out_ref[2 * h + s, 128:144] = pair


def halves(ref):
    keys = ref[:, 0:128].reshape(1024, HD)
    return keys, jnp.concatenate([ref[:, 128:256].reshape(1024, HD), jnp.ones((1024, HD), BF)], axis=1)


def scores_of(q, keys):
    scores = lax.dot_general(q, keys, (((1,), (1,)), ((), ())), preferred_element_type=F32)
    return scores, jnp.max(scores, axis=1, keepdims=True)


def first_half_kernel(q_ref, kv_ref, q_out, sum_out, top_out):
    seq = lax.axis_index("seq")
    keys, vals = halves(kv_ref)
    row = lax.broadcasted_iota(jnp.int32, (32, 128), 0)
    col = lax.broadcasted_iota(jnp.int32, (32, 128), 1)
    pick = (col == (row // 2) % 2 * 64 + (row // 4) * 8 + row % 2 + 6 * seq).astype(F32).astype(BF)
    near = [jnp.dot(pick, q_ref[2 * g + 1 - seq, 0:128], preferred_element_type=F32).astype(BF) for g in range(8)]
    for n in range(10):
        rows = slice(128 * n, 128 * n + 128)
        q = q_ref[2 * n + seq, 0:128] if n < 8 else jnp.concatenate(near[4 * n - 32 : 4 * n - 28], axis=0)
        scores, top = scores_of(q, keys)
        weights = jnp.exp2((scores - top) * SCALE).astype(BF)
        q_out[rows] = q
        sum_out[rows] = jnp.dot(weights, vals, preferred_element_type=F32)
        top_out[rows] = jnp.broadcast_to(top, (128, HD))


def second_half_kernel(q_ref, kv_ref, sum_ref, top_ref, out_ref):
    keys, vals = halves(kv_ref)
    edge = jnp.zeros((32, HD), BF)
    out_ref[0, 0:32] = edge
    out_ref[7, 160:192] = edge
    near = []
    for n in range(10):
        rows = slice(128 * n, 128 * n + 128)
        scores, top = scores_of(q_ref[rows], keys)
        before = top_ref[rows, 0:1]
        top = jnp.maximum(top, before)
        weights = jnp.exp2((scores - top) * SCALE).astype(BF)
        kept = jnp.exp2((before - top) * SCALE)
        both = sum_ref[rows] * kept + jnp.dot(weights, vals, preferred_element_type=F32)
        done = both[:, 0:HD] / both[:, HD : 2 * HD]
        if n >= 8:
            near.append(done)
            continue
        done = done.reshape(2, 8, 8, HD)
        done = jnp.concatenate([done[0], done[1]], axis=1).reshape(128, HD).astype(BF)
        out_ref[n, 32:160] = done
        if n < 7:
            out_ref[n + 1, 0:32] = done[96:128]
        if n > 0:
            out_ref[n - 1, 160:192] = done[0:32]
    none = jnp.zeros((8, HD), F32)
    near = jnp.concatenate([none] + near + [none], axis=0)
    for g in range(8):
        out_ref[g, 192:240] = near[32 * g : 32 * g + 48].astype(BF)


def project_kernel(a_ref, w_ref, out_ref):
    rows = jnp.concatenate([a_ref[h] for h in range(H)], axis=1)
    projected = jnp.dot(rows, w_ref[...], preferred_element_type=F32)
    scale = lax.rsqrt(jnp.mean(projected * projected, axis=1, keepdims=True) + 1e-06)
    out_ref[...] = (projected * scale).astype(BF)


def laid_out(normed):
    seq = lax.axis_index("seq")
    half = normed[0:192].astype(F32).reshape(12, 2, 8, 256)
    near = normed[192:240].astype(F32).reshape(6, 8, 256)
    row = lax.broadcasted_iota(jnp.int32, (12, 8, 256), 1)
    slabs = []
    for x in range(2):
        middle = pltpu.roll(half[:, x], 2, 1)
        ends = [pltpu.roll(near, (8 - 4 * odd - 2 * x) % 8, 1) if odd + x else near for odd in range(2)]
        ends = jnp.stack(ends, axis=1).reshape(12, 8, 256)
        upper = jnp.where(row < 2, jnp.where(seq == 1, ends, 0.0), middle)
        lower = jnp.where((row < 4) & (seq == 0), pltpu.roll(ends, 2, 1), 0.0)
        lower = jnp.where(row < 2, middle, lower)
        slabs.append(jnp.concatenate([upper, lower], axis=1).reshape(192, 256).astype(BF))
    return slabs


def merge_kernel(w_ref, out_ref):
    def both(parts):
        return ((parts[0], parts[1] + parts[2]), (parts[0] + parts[1], parts[2]))

    taps = [[[w_ref[9 * a + 3 * b + c].astype(F32) for c in range(3)] for b in range(3)] for a in range(3)]
    on_z = [[[m for p in both(taps[a][b]) for m in p] for b in range(3)] for a in range(3)]
    for n in range(4):
        on_y = [both([on_z[a][b][n] for b in range(3)]) for a in range(3)]
        for py in range(2):
            for b in range(2):
                on_x = both([on_y[a][py][b] for a in range(3)])
                for px in range(2):
                    for a in range(2):
                        rows = (2 * a + b) * 128
                        out_ref[2 * px + py, rows : rows + 128, n * 128 : (n + 1) * 128] = on_x[px][a].astype(BF)


def shifted(x, by):
    return pltpu.roll(x, by % x.shape[0], 0)


def x_tile():
    return 2 * lax.axis_index("z") + lax.axis_index("core")


def taps(w1_ref, a, b):
    t = 9 * a + 3 * b
    return jnp.concatenate([w1_ref[t], w1_ref[t + 1], w1_ref[t + 2]], axis=1)


def own_conv_kernel(own_ref, w1_ref, out_ref):
    slabs = laid_out(own_ref[...])
    for x in range(4):
        total = jnp.zeros((160, 384), F32)
        for a in range(3):
            if 2 <= x + a < 4:
                for b in range(3):
                    part = slabs[x + a - 2][16 * b : 16 * b + 160]
                    total = total + jnp.dot(part, taps(w1_ref, a, b), preferred_element_type=F32)
        out_ref[x] = total


def side(at_left, slabs, own_ref, w1_ref):
    gx, gy, seq = x_tile(), lax.axis_index("gy"), lax.axis_index("seq")
    row = lax.broadcasted_iota(jnp.int32, (160, 128), 0)
    at_z = seq * 8 - 1 + row % 16
    at_y = gy * 8 - 1 + row // 16
    inside = (at_y >= 0) & (at_y < 64) & (at_z >= 0) & (at_z < 16)
    first_tap = jnp.where(at_left, 0, 1)
    outer = [(slabs[0], first_tap), (slabs[1], first_tap + 1)]
    inner = [(jnp.where(at_left, slabs[1], slabs[0]), jnp.where(at_left, 0, 2))]
    results = []
    for x, terms in ((jnp.where(at_left, 0, 3), outer), (jnp.where(at_left, 1, 2), inner)):
        total = own_ref[x]
        for slab, a in terms:
            for b in range(3):
                total = total + jnp.dot(slab[16 * b : 16 * b + 160], taps(w1_ref, a, b), preferred_element_type=F32)
        first = total[:, 0:128] + shifted(total[:, 128:256], -1) + shifted(total[:, 256:384], -2)
        value = first / (1.0 + jnp.exp(-first))
        at_x = gx * 2 - 1 + x
        results.append((x, jnp.where(inside & (at_x >= 0) & (at_x < 32), value, 0.0).astype(BF)))
    return results


def near_conv_kernel(near_ref, own_ref, w1_ref, out_ref):
    at_left = lax.axis_index("core") == 1
    slabs = laid_out(near_ref[...])
    for n, (_, rows) in enumerate(side(at_left, slabs, own_ref, w1_ref)):
        out_ref[n] = rows


def conv_kernel(own_ref, done_ref, far_ref, w1_ref, w2_ref, out_hbm, hidden, field, ready, sems):
    gx = x_tile()
    at_left = lax.axis_index("core") == 0
    there = jnp.where(at_left, gx > 0, gx < 15)
    slabs = [jnp.where(there, slab, jnp.zeros_like(slab)) for slab in laid_out(far_ref[...])]
    hidden[jnp.where(at_left, 3, 0)] = done_ref[0]
    hidden[jnp.where(at_left, 2, 1)] = done_ref[1]
    for x, rows in side(at_left, slabs, own_ref, w1_ref):
        hidden[x] = rows
    copies = []
    for px in range(2):
        for py in range(2):
            rows = [
                [hidden[i + px + a, 16 * (py + b) : 16 * (py + b) + 128] for a in range(2) for b in range(2)]
                for i in range(2)
            ]
            rows = jnp.concatenate([jnp.concatenate(parts, axis=1) for parts in rows], axis=0)
            parts = jnp.dot(rows, w2_ref[2 * px + py], preferred_element_type=F32)
            even = parts[:, 0:128] + shifted(parts[:, 128:256], -1)
            odd = shifted(parts[:, 256:384], -1) + shifted(parts[:, 384:512], -2)
            for pz, part in ((0, even), (1, odd)):
                part = part.reshape(2, 8, 16, 128)
                for i in range(2):
                    for j in range(8):
                        field[2 * i + px, 2 * j + py, pl.ds(pz, 8, stride=2), :] = part[i, j, 0:8]
        for x in (px, px + 2):
            ready[x] = field[x].astype(BF)
            copies.append(pltpu.make_async_copy(ready.at[x], out_hbm.at[x], sems.at[x]))
            copies[-1].start()
    for copy in copies:
        copy.wait()


def body(queries, keys, values, w_out, conv_first, conv_second):
    sent = call(
        pack_kernel,
        [(16, 144, HD)],
        [BF],
        [HB] * 3,
        [
            pltpu.VMEM((2, 64, H * HD), BF),
            pltpu.VMEM((8, H * HD), BF),
            pltpu.VMEM((8, H * HD), BF),
            pltpu.SemaphoreType.DMA((3,)),
        ],
    )(*(pltpu.with_memory_space_constraint(a, pltpu.HBM) for a in (queries.reshape(2, 64, H * HD), keys, values)))
    got = lax.all_to_all(sent, ("gy", "seq"), 0, 0, tiled=True)
    pair = got[:, 128:144].reshape(16, 2, 8, HD).transpose(1, 0, 2, 3).reshape(1, 256, HD)
    own = lax.all_to_all(jnp.broadcast_to(pair, (8, 256, HD)), "z", 0, 0, tiled=True)
    other = lax.ppermute(own, "core", [(0, 1), (1, 0)])
    half = call(first_half_kernel, [(1280, HD), (1280, 2 * HD), (1280, HD)], [BF, F32, F32], [VM, VM])
    q, summed, top = half(got, own)
    attended = call(second_half_kernel, [(8, 240, HD)], [BF], [VM] * 4)(q, other, summed, top)
    back = lax.all_to_all(attended, "gy", 0, 0, tiled=True)
    normed = call(project_kernel, [(240, 256)], [BF], [VM, VM])(back, w_out)
    far = lax.ppermute(normed, ("z", "core"), [(i, (i - 1 + 2 * (i % 2)) % 16) for i in range(16)])
    near = lax.ppermute(normed, "core", [(0, 1), (1, 0)])
    w1 = conv_first.reshape(27, 256, 128)
    merged = call(merge_kernel, [(4, 512, 512)], [BF], [VM])(conv_second.reshape(27, 128, 128))
    own_part = call(own_conv_kernel, [(4, 160, 384)], [F32], [VM, VM])(normed, w1)
    done = call(near_conv_kernel, [(2, 160, 128)], [BF], [VM] * 3)(near, own_part, w1)
    scratch = [
        pltpu.VMEM((4, 160, 128), BF),
        pltpu.VMEM((4, 16, 16, 128), F32),
        pltpu.VMEM((4, 16, 16, 128), BF),
        pltpu.SemaphoreType.DMA((4,)),
    ]
    final = call(conv_kernel, [(4, 16, 16, 128)], [BF], [VM] * 5, scratch, HB)
    return final(own_part, done, far, w1, merged)


def solution(mesh):
    cut = Mesh(mesh.devices.reshape(8, 2, 8, 2), ("z", "core", "gy", "seq"))
    tokens = P(("z", "core", "gy", "seq"), None)
    voxels = P(("z", "core"), "gy", "seq", None)
    return jax.shard_map(
        body, mesh=cut, in_specs=(voxels, tokens, tokens, P(), P(), P()), out_specs=voxels, check_vma=False
    )
```

```python
import jax
import jax.numpy as jnp
from jax import lax
from jax.experimental import pallas as pl
from jax.experimental.pallas import tpu as pltpu
from jax.sharding import Mesh, PartitionSpec as P

H = 8
HD = 128
BF = jnp.bfloat16
F32 = jnp.float32
VM = pl.BlockSpec(memory_space=pltpu.VMEM)
HB = pl.BlockSpec(memory_space=pltpu.HBM)
SCALE = HD**-0.5 * 1.4426950408889634


def call(kernel, shapes, dtypes, in_specs, scratch=(), out_spec=VM):
    outs = [jax.ShapeDtypeStruct(shape, dtype) for shape, dtype in zip(shapes, dtypes)]
    one = len(outs) == 1
    return pl.pallas_call(
        kernel,
        out_shape=outs[0] if one else outs,
        in_specs=in_specs,
        out_specs=out_spec if one else [VM] * len(outs),
        scratch_shapes=list(scratch),
        compiler_params=pltpu.CompilerParams(vmem_limit_bytes=24 * 1024 * 1024),
        cost_estimate=pl.CostEstimate(flops=10**6, bytes_accessed=10000, transcendentals=0),
    )


def slot(tile, half):
    return 4 * (tile // 2) + 2 * half + tile % 2


def pack_kernel(q_hbm, k_hbm, v_hbm, out_ref, q_ref, k_ref, v_ref, sems):
    copies = [
        pltpu.make_async_copy(src, dst, sems.at[i])
        for i, (src, dst) in enumerate(((q_hbm, q_ref), (k_hbm, k_ref), (v_hbm, v_ref)))
    ]
    for copy in copies:
        copy.start()
    for copy in copies:
        copy.wait()
    for h in range(H):
        cols = slice(h * HD, (h + 1) * HD)
        pair = jnp.concatenate([k_ref[:, cols].astype(F32), v_ref[:, cols].astype(F32)], axis=0).astype(BF)
        for s in range(2):
            out_ref[slot(h, s), 0:64] = q_ref[0, :, cols]
            out_ref[slot(h, s), 64:128] = q_ref[1, :, cols]
            out_ref[slot(h, s), 128:144] = pair


def halves(ref):
    keys = ref[:, 0:128].reshape(1024, HD)
    return keys, jnp.concatenate([ref[:, 128:256].reshape(1024, HD), jnp.ones((1024, HD), BF)], axis=1)


def scores_of(q, keys):
    scores = lax.dot_general(q, keys, (((1,), (1,)), ((), ())), preferred_element_type=F32)
    return scores, jnp.max(scores, axis=1, keepdims=True)


def first_half_kernel(q_ref, kv_ref, q_out, sum_out, top_out):
    seq = lax.axis_index("seq")
    keys, vals = halves(kv_ref)
    row = lax.broadcasted_iota(jnp.int32, (32, 128), 0)
    col = lax.broadcasted_iota(jnp.int32, (32, 128), 1)
    pick = (col == (row // 2) % 2 * 64 + (row // 4) * 8 + row % 2 + 6 * seq).astype(F32).astype(BF)
    near = [jnp.dot(pick, q_ref[slot(g, 1 - seq), 0:128], preferred_element_type=F32).astype(BF) for g in range(8)]
    for n in range(10):
        rows = slice(128 * n, 128 * n + 128)
        q = q_ref[slot(n, seq), 0:128] if n < 8 else jnp.concatenate(near[4 * n - 32 : 4 * n - 28], axis=0)
        scores, top = scores_of(q, keys)
        weights = jnp.exp2((scores - top) * SCALE).astype(BF)
        q_out[rows] = q
        sum_out[rows] = jnp.dot(weights, vals, preferred_element_type=F32)
        top_out[rows] = jnp.broadcast_to(top, (128, HD))


def second_half_kernel(q_ref, kv_ref, sum_ref, top_ref, out_ref):
    keys, vals = halves(kv_ref)
    edge = jnp.zeros((32, HD), BF)
    out_ref[0, 0:32] = edge
    out_ref[7, 160:192] = edge
    near = []
    for n in range(10):
        rows = slice(128 * n, 128 * n + 128)
        scores, top = scores_of(q_ref[rows], keys)
        before = top_ref[rows, 0:1]
        top = jnp.maximum(top, before)
        weights = jnp.exp2((scores - top) * SCALE).astype(BF)
        kept = jnp.exp2((before - top) * SCALE)
        both = sum_ref[rows] * kept + jnp.dot(weights, vals, preferred_element_type=F32)
        done = both[:, 0:HD] / both[:, HD : 2 * HD]
        if n >= 8:
            near.append(done)
            continue
        done = done.reshape(2, 8, 8, HD)
        done = jnp.concatenate([done[0], done[1]], axis=1).reshape(128, HD).astype(BF)
        out_ref[n, 32:160] = done
        if n < 7:
            out_ref[n + 1, 0:32] = done[96:128]
        if n > 0:
            out_ref[n - 1, 160:192] = done[0:32]
    none = jnp.zeros((8, HD), F32)
    near = jnp.concatenate([none] + near + [none], axis=0)
    for g in range(8):
        out_ref[g, 192:240] = near[32 * g : 32 * g + 48].astype(BF)


def project_kernel(a_ref, w_ref, out_ref):
    rows = jnp.concatenate([a_ref[h] for h in range(H)], axis=1)
    projected = jnp.dot(rows, w_ref[...], preferred_element_type=F32)
    scale = lax.rsqrt(jnp.mean(projected * projected, axis=1, keepdims=True) + 1e-06)
    out_ref[...] = (projected * scale).astype(BF)


def laid_out(normed):
    seq = lax.axis_index("seq")
    half = normed[0:192].astype(F32).reshape(12, 2, 8, 256)
    near = normed[192:240].astype(F32).reshape(6, 8, 256)
    row = lax.broadcasted_iota(jnp.int32, (12, 8, 256), 1)
    slabs = []
    for x in range(2):
        middle = pltpu.roll(half[:, x], 2, 1)
        ends = [pltpu.roll(near, (8 - 4 * odd - 2 * x) % 8, 1) if odd + x else near for odd in range(2)]
        ends = jnp.stack(ends, axis=1).reshape(12, 8, 256)
        upper = jnp.where(row < 2, jnp.where(seq == 1, ends, 0.0), middle)
        lower = jnp.where((row < 4) & (seq == 0), pltpu.roll(ends, 2, 1), 0.0)
        lower = jnp.where(row < 2, middle, lower)
        slabs.append(jnp.concatenate([upper, lower], axis=1).reshape(192, 256).astype(BF))
    return slabs


def merge_kernel(w_ref, out_ref):
    def both(parts):
        return ((parts[0], parts[1] + parts[2]), (parts[0] + parts[1], parts[2]))

    taps = [[[w_ref[9 * a + 3 * b + c].astype(F32) for c in range(3)] for b in range(3)] for a in range(3)]
    on_z = [[[m for p in both(taps[a][b]) for m in p] for b in range(3)] for a in range(3)]
    for n in range(4):
        on_y = [both([on_z[a][b][n] for b in range(3)]) for a in range(3)]
        for py in range(2):
            for b in range(2):
                on_x = both([on_y[a][py][b] for a in range(3)])
                for px in range(2):
                    for a in range(2):
                        rows = (2 * a + b) * 128
                        out_ref[2 * px + py, rows : rows + 128, n * 128 : (n + 1) * 128] = on_x[px][a].astype(BF)


def shifted(x, by):
    return pltpu.roll(x, by % x.shape[0], 0)


def x_tile():
    return 2 * lax.axis_index("z") + lax.axis_index("core")


def taps(w1_ref, a, b):
    t = 9 * a + 3 * b
    return jnp.concatenate([w1_ref[t], w1_ref[t + 1], w1_ref[t + 2]], axis=1)


def own_conv_kernel(own_ref, w1_ref, out_ref):
    slabs = laid_out(own_ref[...])
    for x in range(4):
        total = jnp.zeros((160, 384), F32)
        for a in range(3):
            if 2 <= x + a < 4:
                for b in range(3):
                    part = slabs[x + a - 2][16 * b : 16 * b + 160]
                    total = total + jnp.dot(part, taps(w1_ref, a, b), preferred_element_type=F32)
        out_ref[x] = total


def side(at_left, slabs, own_ref, w1_ref):
    gx, gy, seq = x_tile(), 2 * lax.axis_index("chip_x") + lax.axis_index("low_y"), lax.axis_index("seq")
    row = lax.broadcasted_iota(jnp.int32, (160, 128), 0)
    at_z = seq * 8 - 1 + row % 16
    at_y = gy * 8 - 1 + row // 16
    inside = (at_y >= 0) & (at_y < 64) & (at_z >= 0) & (at_z < 16)
    first_tap = jnp.where(at_left, 0, 1)
    outer = [(slabs[0], first_tap), (slabs[1], first_tap + 1)]
    inner = [(jnp.where(at_left, slabs[1], slabs[0]), jnp.where(at_left, 0, 2))]
    results = []
    for x, terms in ((jnp.where(at_left, 0, 3), outer), (jnp.where(at_left, 1, 2), inner)):
        total = own_ref[x]
        for slab, a in terms:
            for b in range(3):
                total = total + jnp.dot(slab[16 * b : 16 * b + 160], taps(w1_ref, a, b), preferred_element_type=F32)
        first = total[:, 0:128] + shifted(total[:, 128:256], -1) + shifted(total[:, 256:384], -2)
        value = first / (1.0 + jnp.exp(-first))
        at_x = gx * 2 - 1 + x
        results.append((x, jnp.where(inside & (at_x >= 0) & (at_x < 32), value, 0.0).astype(BF)))
    return results


def near_conv_kernel(near_ref, own_ref, w1_ref, out_ref):
    at_left = lax.axis_index("core") == 1
    slabs = laid_out(near_ref[...])
    for n, (_, rows) in enumerate(side(at_left, slabs, own_ref, w1_ref)):
        out_ref[n] = rows


def conv_kernel(own_ref, done_ref, far_ref, w1_ref, w2_ref, out_hbm, hidden, field, ready, sems):
    gx = x_tile()
    at_left = lax.axis_index("core") == 0
    there = jnp.where(at_left, gx > 0, gx < 15)
    slabs = [jnp.where(there, slab, jnp.zeros_like(slab)) for slab in laid_out(far_ref[...])]
    hidden[jnp.where(at_left, 3, 0)] = done_ref[0]
    hidden[jnp.where(at_left, 2, 1)] = done_ref[1]
    for x, rows in side(at_left, slabs, own_ref, w1_ref):
        hidden[x] = rows
    copies = []
    for px in range(2):
        for py in range(2):
            rows = [
                [hidden[i + px + a, 16 * (py + b) : 16 * (py + b) + 128] for a in range(2) for b in range(2)]
                for i in range(2)
            ]
            rows = jnp.concatenate([jnp.concatenate(parts, axis=1) for parts in rows], axis=0)
            parts = jnp.dot(rows, w2_ref[2 * px + py], preferred_element_type=F32)
            even = parts[:, 0:128] + shifted(parts[:, 128:256], -1)
            odd = shifted(parts[:, 256:384], -1) + shifted(parts[:, 384:512], -2)
            for pz, part in ((0, even), (1, odd)):
                part = part.reshape(2, 8, 16, 128)
                for i in range(2):
                    for j in range(8):
                        field[2 * i + px, 2 * j + py, pl.ds(pz, 8, stride=2), :] = part[i, j, 0:8]
        for x in (px, px + 2):
            ready[x] = field[x].astype(BF)
            copies.append(pltpu.make_async_copy(ready.at[x], out_hbm.at[x], sems.at[x]))
            copies[-1].start()
    for copy in copies:
        copy.wait()


def body(queries, keys, values, w_out, conv_first, conv_second):
    sent = call(
        pack_kernel,
        [(16, 144, HD)],
        [BF],
        [HB] * 3,
        [
            pltpu.VMEM((2, 64, H * HD), BF),
            pltpu.VMEM((8, H * HD), BF),
            pltpu.VMEM((8, H * HD), BF),
            pltpu.SemaphoreType.DMA((3,)),
        ],
    )(*(pltpu.with_memory_space_constraint(a, pltpu.HBM) for a in (queries.reshape(2, 64, H * HD), keys, values)))
    got = lax.all_to_all(sent, ("chip_x", "seq", "low_y"), 0, 0, tiled=True)
    pair = got[:, 128:144].reshape(16, 2, 8, HD).transpose(1, 0, 2, 3).reshape(1, 256, HD)
    own = lax.all_to_all(jnp.broadcast_to(pair, (8, 256, HD)), "z", 0, 0, tiled=True)
    other = lax.ppermute(own, "core", [(0, 1), (1, 0)])
    half = call(first_half_kernel, [(1280, HD), (1280, 2 * HD), (1280, HD)], [BF, F32, F32], [VM, VM])
    q, summed, top = half(got, own)
    attended = call(second_half_kernel, [(8, 240, HD)], [BF], [VM] * 4)(q, other, summed, top)
    back = lax.all_to_all(attended, ("chip_x", "low_y"), 0, 0, tiled=True)
    normed = call(project_kernel, [(240, 256)], [BF], [VM, VM])(back, w_out)
    far = lax.ppermute(normed, ("z", "core"), [(i, (i - 1 + 2 * (i % 2)) % 16) for i in range(16)])
    near = lax.ppermute(normed, "core", [(0, 1), (1, 0)])
    w1 = conv_first.reshape(27, 256, 128)
    merged = call(merge_kernel, [(4, 512, 512)], [BF], [VM])(conv_second.reshape(27, 128, 128))
    own_part = call(own_conv_kernel, [(4, 160, 384)], [F32], [VM, VM])(normed, w1)
    done = call(near_conv_kernel, [(2, 160, 128)], [BF], [VM] * 3)(near, own_part, w1)
    scratch = [
        pltpu.VMEM((4, 160, 128), BF),
        pltpu.VMEM((4, 16, 16, 128), F32),
        pltpu.VMEM((4, 16, 16, 128), BF),
        pltpu.SemaphoreType.DMA((4,)),
    ]
    final = call(conv_kernel, [(4, 16, 16, 128)], [BF], [VM] * 5, scratch, HB)
    return final(own_part, done, far, w1, merged)


def solution(mesh):
    cut = Mesh(mesh.devices.reshape(8, 2, 4, 2, 2), ("z", "core", "chip_x", "low_y", "seq"))
    tokens = P(("z", "core", "chip_x", "low_y", "seq"), None)
    voxels = P(("z", "core"), ("chip_x", "low_y"), "seq", None)
    return jax.shard_map(
        body, mesh=cut, in_specs=(voxels, tokens, tokens, P(), P(), P()), out_specs=voxels, check_vma=False
    )
```

```python
import jax
import jax.numpy as jnp
from jax import lax
from jax.experimental import pallas as pl
from jax.experimental.pallas import tpu as pltpu
from jax.sharding import Mesh, PartitionSpec as P

H = 8
HD = 128
BF = jnp.bfloat16
F32 = jnp.float32
VM = pl.BlockSpec(memory_space=pltpu.VMEM)
HB = pl.BlockSpec(memory_space=pltpu.HBM)
SCALE = HD**-0.5 * 1.4426950408889634


def call(kernel, shapes, dtypes, in_specs, scratch=(), out_spec=VM):
    outs = [jax.ShapeDtypeStruct(shape, dtype) for shape, dtype in zip(shapes, dtypes)]
    one = len(outs) == 1
    return pl.pallas_call(
        kernel,
        out_shape=outs[0] if one else outs,
        in_specs=in_specs,
        out_specs=out_spec if one else [VM] * len(outs),
        scratch_shapes=list(scratch),
        compiler_params=pltpu.CompilerParams(vmem_limit_bytes=24 * 1024 * 1024),
        cost_estimate=pl.CostEstimate(flops=10**6, bytes_accessed=10000, transcendentals=0),
    )


def slot(tile, half):
    return 4 * (tile // 2) + 2 * half + tile % 2


def pack_kernel(q_hbm, k_hbm, v_hbm, out_ref, q_ref, k_ref, v_ref, sems):
    copies = [
        pltpu.make_async_copy(src, dst, sems.at[i])
        for i, (src, dst) in enumerate(((q_hbm, q_ref), (k_hbm, k_ref), (v_hbm, v_ref)))
    ]
    for copy in copies:
        copy.start()
    for copy in copies:
        copy.wait()
    for h in range(H):
        cols = slice(h * HD, (h + 1) * HD)
        pair = jnp.concatenate([k_ref[:, cols].astype(F32), v_ref[:, cols].astype(F32)], axis=0).astype(BF)
        for s in range(2):
            out_ref[slot(h, s), 0:64] = q_ref[s, :, cols]
            out_ref[slot(h, s), 64:80] = pair


def halves(ref):
    keys = ref[:, 0:128].reshape(1024, HD)
    return keys, jnp.concatenate([ref[:, 128:256].reshape(1024, HD), jnp.ones((1024, HD), BF)], axis=1)


def scores_of(q, keys):
    scores = lax.dot_general(q, keys, (((1,), (1,)), ((), ())), preferred_element_type=F32)
    return scores, jnp.max(scores, axis=1, keepdims=True)


def queries_of(q_ref, n):
    return jnp.concatenate([q_ref[slot(n, 0), 0:64], q_ref[slot(n, 1), 0:64]], axis=0)


def first_half_kernel(q_ref, kv_ref, sum_out, top_out):
    keys, vals = halves(kv_ref)
    for n in range(8):
        rows = slice(128 * n, 128 * n + 128)
        scores, top = scores_of(queries_of(q_ref, n), keys)
        weights = jnp.exp2((scores - top) * SCALE).astype(BF)
        sum_out[rows] = jnp.dot(weights, vals, preferred_element_type=F32)
        top_out[rows] = jnp.broadcast_to(top, (128, HD))


def second_half_kernel(q_ref, kv_ref, sum_ref, top_ref, out_ref):
    keys, vals = halves(kv_ref)
    edge = jnp.zeros((16, HD), BF)
    for s in range(2):
        out_ref[slot(0, s), 0:16] = edge
        out_ref[slot(7, s), 80:96] = edge
    for n in range(8):
        rows = slice(128 * n, 128 * n + 128)
        scores, top = scores_of(queries_of(q_ref, n), keys)
        before = top_ref[rows, 0:1]
        top = jnp.maximum(top, before)
        weights = jnp.exp2((scores - top) * SCALE).astype(BF)
        kept = jnp.exp2((before - top) * SCALE)
        both = sum_ref[rows] * kept + jnp.dot(weights, vals, preferred_element_type=F32)
        done = (both[:, 0:HD] / both[:, HD : 2 * HD]).astype(BF)
        for s in range(2):
            half = done[64 * s : 64 * s + 64]
            out_ref[slot(n, s), 16:80] = half
            if n < 7:
                out_ref[slot(n + 1, s), 0:16] = half[48:64]
            if n > 0:
                out_ref[slot(n - 1, s), 80:96] = half[0:16]
    row = lax.broadcasted_iota(jnp.int32, (32, 96), 0)
    col = lax.broadcasted_iota(jnp.int32, (32, 96), 1)
    for s in range(2):
        pick = ((col == (row // 2) * 8 + row % 2 + 6 * s) & (row < 24)).astype(F32).astype(BF)
        for n in range(8):
            other = out_ref[slot(n, 1 - s), 0:96]
            out_ref[slot(n, s), 96:128] = jnp.dot(pick, other, preferred_element_type=F32).astype(BF)


def project_kernel(a_ref, w_ref, out_ref):
    rows = [jnp.concatenate([a_ref[slot(h, x)] for h in range(H)], axis=1) for x in range(2)]
    projected = jnp.dot(jnp.concatenate(rows, axis=0), w_ref[...], preferred_element_type=F32)
    scale = lax.rsqrt(jnp.mean(projected * projected, axis=1, keepdims=True) + 1e-06)
    out_ref[...] = (projected * scale).astype(BF)


def laid_out(normed):
    seq = lax.axis_index("seq")
    row = lax.broadcasted_iota(jnp.int32, (12, 8, 256), 1)
    slabs = []
    for x in range(2):
        middle = pltpu.roll(normed[128 * x : 128 * x + 96].astype(F32).reshape(12, 8, 256), 2, 1)
        near = normed[128 * x + 96 : 128 * x + 128].astype(F32).reshape(4, 8, 256)[0:3]
        ends = [pltpu.roll(near, 8 - 2 * k, 1) if k else near for k in range(4)]
        ends = jnp.stack(ends, axis=1).reshape(12, 8, 256)
        upper = jnp.where(row < 2, jnp.where(seq == 1, ends, 0.0), middle)
        lower = jnp.where((row < 4) & (seq == 0), pltpu.roll(ends, 2, 1), 0.0)
        lower = jnp.where(row < 2, middle, lower)
        slabs.append(jnp.concatenate([upper, lower], axis=1).reshape(192, 256).astype(BF))
    return slabs


def merge_kernel(w_ref, out_ref):
    def both(parts):
        return ((parts[0], parts[1] + parts[2]), (parts[0] + parts[1], parts[2]))

    taps = [[[w_ref[9 * a + 3 * b + c].astype(F32) for c in range(3)] for b in range(3)] for a in range(3)]
    on_z = [[[m for p in both(taps[a][b]) for m in p] for b in range(3)] for a in range(3)]
    for n in range(4):
        on_y = [both([on_z[a][b][n] for b in range(3)]) for a in range(3)]
        for py in range(2):
            for b in range(2):
                on_x = both([on_y[a][py][b] for a in range(3)])
                for px in range(2):
                    for a in range(2):
                        rows = (2 * a + b) * 128
                        out_ref[2 * px + py, rows : rows + 128, n * 128 : (n + 1) * 128] = on_x[px][a].astype(BF)


def shifted(x, by):
    return pltpu.roll(x, by % x.shape[0], 0)


def x_tile():
    return 2 * lax.axis_index("z") + lax.axis_index("core")


def taps(w1_ref, a, b):
    t = 9 * a + 3 * b
    return jnp.concatenate([w1_ref[t], w1_ref[t + 1], w1_ref[t + 2]], axis=1)


def own_conv_kernel(own_ref, w1_ref, out_ref):
    slabs = laid_out(own_ref[...])
    for x in range(4):
        total = jnp.zeros((160, 384), F32)
        for a in range(3):
            if 2 <= x + a < 4:
                for b in range(3):
                    part = slabs[x + a - 2][16 * b : 16 * b + 160]
                    total = total + jnp.dot(part, taps(w1_ref, a, b), preferred_element_type=F32)
        out_ref[x] = total


def side(at_left, slabs, own_ref, w1_ref):
    gx, gy, seq = x_tile(), 2 * lax.axis_index("chip_x") + lax.axis_index("low_y"), lax.axis_index("seq")
    row = lax.broadcasted_iota(jnp.int32, (160, 128), 0)
    at_z = seq * 8 - 1 + row % 16
    at_y = gy * 8 - 1 + row // 16
    inside = (at_y >= 0) & (at_y < 64) & (at_z >= 0) & (at_z < 16)
    first_tap = jnp.where(at_left, 0, 1)
    outer = [(slabs[0], first_tap), (slabs[1], first_tap + 1)]
    inner = [(jnp.where(at_left, slabs[1], slabs[0]), jnp.where(at_left, 0, 2))]
    results = []
    for x, terms in ((jnp.where(at_left, 0, 3), outer), (jnp.where(at_left, 1, 2), inner)):
        total = own_ref[x]
        for slab, a in terms:
            for b in range(3):
                total = total + jnp.dot(slab[16 * b : 16 * b + 160], taps(w1_ref, a, b), preferred_element_type=F32)
        first = total[:, 0:128] + shifted(total[:, 128:256], -1) + shifted(total[:, 256:384], -2)
        value = first / (1.0 + jnp.exp(-first))
        at_x = gx * 2 - 1 + x
        results.append((x, jnp.where(inside & (at_x >= 0) & (at_x < 32), value, 0.0).astype(BF)))
    return results


def near_conv_kernel(near_ref, own_ref, w1_ref, out_ref):
    at_left = lax.axis_index("core") == 1
    slabs = laid_out(near_ref[...])
    for n, (_, rows) in enumerate(side(at_left, slabs, own_ref, w1_ref)):
        out_ref[n] = rows


def conv_kernel(own_ref, done_ref, far_ref, w1_ref, w2_ref, out_hbm, hidden, field, ready, sems):
    gx = x_tile()
    at_left = lax.axis_index("core") == 0
    there = jnp.where(at_left, gx > 0, gx < 15)
    slabs = [jnp.where(there, slab, jnp.zeros_like(slab)) for slab in laid_out(far_ref[...])]
    hidden[jnp.where(at_left, 3, 0)] = done_ref[0]
    hidden[jnp.where(at_left, 2, 1)] = done_ref[1]
    for x, rows in side(at_left, slabs, own_ref, w1_ref):
        hidden[x] = rows
    copies = []
    for px in range(2):
        for py in range(2):
            rows = [
                [hidden[i + px + a, 16 * (py + b) : 16 * (py + b) + 128] for a in range(2) for b in range(2)]
                for i in range(2)
            ]
            rows = jnp.concatenate([jnp.concatenate(parts, axis=1) for parts in rows], axis=0)
            parts = jnp.dot(rows, w2_ref[2 * px + py], preferred_element_type=F32)
            even = parts[:, 0:128] + shifted(parts[:, 128:256], -1)
            odd = shifted(parts[:, 256:384], -1) + shifted(parts[:, 384:512], -2)
            for pz, part in ((0, even), (1, odd)):
                part = part.reshape(2, 8, 16, 128)
                for i in range(2):
                    for j in range(8):
                        field[2 * i + px, 2 * j + py, pl.ds(pz, 8, stride=2), :] = part[i, j, 0:8]
        for x in (px, px + 2):
            ready[x] = field[x].astype(BF)
            copies.append(pltpu.make_async_copy(ready.at[x], out_hbm.at[x], sems.at[x]))
            copies[-1].start()
    for copy in copies:
        copy.wait()


def body(queries, keys, values, w_out, conv_first, conv_second):
    sent = call(
        pack_kernel,
        [(16, 80, HD)],
        [BF],
        [HB] * 3,
        [
            pltpu.VMEM((2, 64, H * HD), BF),
            pltpu.VMEM((8, H * HD), BF),
            pltpu.VMEM((8, H * HD), BF),
            pltpu.SemaphoreType.DMA((3,)),
        ],
    )(*(pltpu.with_memory_space_constraint(a, pltpu.HBM) for a in (queries.reshape(2, 64, H * HD), keys, values)))
    got = lax.all_to_all(sent, ("chip_x", "seq", "low_y"), 0, 0, tiled=True)
    pair = got[:, 64:80].reshape(16, 2, 8, HD).transpose(1, 0, 2, 3).reshape(1, 256, HD)
    own = lax.all_to_all(jnp.broadcast_to(pair, (8, 256, HD)), "z", 0, 0, tiled=True)
    other = lax.ppermute(own, "core", [(0, 1), (1, 0)])
    summed, top = call(first_half_kernel, [(1024, 2 * HD), (1024, HD)], [F32, F32], [VM, VM])(got, own)
    attended = call(second_half_kernel, [(16, 128, HD)], [BF], [VM] * 4)(got, other, summed, top)
    back = lax.all_to_all(attended, ("chip_x", "seq", "low_y"), 0, 0, tiled=True)
    normed = call(project_kernel, [(256, 256)], [BF], [VM, VM])(back, w_out)
    far = lax.ppermute(normed, ("z", "core"), [(i, (i - 1 + 2 * (i % 2)) % 16) for i in range(16)])
    near = lax.ppermute(normed, "core", [(0, 1), (1, 0)])
    w1 = conv_first.reshape(27, 256, 128)
    merged = call(merge_kernel, [(4, 512, 512)], [BF], [VM])(conv_second.reshape(27, 128, 128))
    own_part = call(own_conv_kernel, [(4, 160, 384)], [F32], [VM, VM])(normed, w1)
    done = call(near_conv_kernel, [(2, 160, 128)], [BF], [VM] * 3)(near, own_part, w1)
    scratch = [
        pltpu.VMEM((4, 160, 128), BF),
        pltpu.VMEM((4, 16, 16, 128), F32),
        pltpu.VMEM((4, 16, 16, 128), BF),
        pltpu.SemaphoreType.DMA((4,)),
    ]
    final = call(conv_kernel, [(4, 16, 16, 128)], [BF], [VM] * 5, scratch, HB)
    return final(own_part, done, far, w1, merged)


def solution(mesh):
    cut = Mesh(mesh.devices.reshape(8, 2, 4, 2, 2), ("z", "core", "chip_x", "low_y", "seq"))
    tokens = P(("z", "core", "chip_x", "low_y", "seq"), None)
    voxels = P(("z", "core"), ("chip_x", "low_y"), "seq", None)
    return jax.shard_map(
        body, mesh=cut, in_specs=(voxels, tokens, tokens, P(), P(), P()), out_specs=voxels, check_vma=False
    )
```

```python
import jax
import jax.numpy as jnp
from jax import lax
from jax.experimental import pallas as pl
from jax.experimental.pallas import tpu as pltpu
from jax.sharding import Mesh, PartitionSpec as P

H = 8
HD = 128
BF = jnp.bfloat16
F32 = jnp.float32
VM = pl.BlockSpec(memory_space=pltpu.VMEM)
HB = pl.BlockSpec(memory_space=pltpu.HBM)
SCALE = HD**-0.5 * 1.4426950408889634


def call(kernel, shapes, dtypes, in_specs, scratch=(), out_spec=VM):
    outs = [jax.ShapeDtypeStruct(shape, dtype) for shape, dtype in zip(shapes, dtypes)]
    one = len(outs) == 1
    return pl.pallas_call(
        kernel,
        out_shape=outs[0] if one else outs,
        in_specs=in_specs,
        out_specs=out_spec if one else [VM] * len(outs),
        scratch_shapes=list(scratch),
        compiler_params=pltpu.CompilerParams(vmem_limit_bytes=24 * 1024 * 1024),
        cost_estimate=pl.CostEstimate(flops=10**6, bytes_accessed=10000, transcendentals=0),
    )


def slot(tile, half):
    return 4 * (tile // 2) + 2 * half + tile % 2


def pack_kernel(q_hbm, k_hbm, v_hbm, out_ref, q_ref, k_ref, v_ref, sems):
    copies = [
        pltpu.make_async_copy(src, dst, sems.at[i])
        for i, (src, dst) in enumerate(((q_hbm, q_ref), (k_hbm, k_ref), (v_hbm, v_ref)))
    ]
    for copy in copies:
        copy.start()
    for copy in copies:
        copy.wait()
    for h in range(H):
        cols = slice(h * HD, (h + 1) * HD)
        pair = jnp.concatenate([k_ref[:, cols].astype(F32), v_ref[:, cols].astype(F32)], axis=0).astype(BF)
        for s in range(2):
            out_ref[slot(h, s), 0:64] = q_ref[s, :, cols]
            out_ref[slot(h, s), 64:80] = pair


def halves(ref):
    keys = ref[:, 0:128].reshape(1024, HD)
    return keys, jnp.concatenate([ref[:, 128:256].reshape(1024, HD), jnp.ones((1024, HD), BF)], axis=1)


def scores_of(q, keys):
    scores = lax.dot_general(q, keys, (((1,), (1,)), ((), ())), preferred_element_type=F32)
    return scores, jnp.max(scores, axis=1, keepdims=True)


def queries_of(q_ref, n):
    return jnp.concatenate([q_ref[slot(n, 0), 0:64], q_ref[slot(n, 1), 0:64]], axis=0)


def first_half_kernel(q_ref, kv_ref, sum_out, top_out):
    keys, vals = halves(kv_ref)
    for n in range(8):
        rows = slice(128 * n, 128 * n + 128)
        scores, top = scores_of(queries_of(q_ref, n), keys)
        weights = jnp.exp2((scores - top) * SCALE).astype(BF)
        sum_out[rows] = jnp.dot(weights, vals, preferred_element_type=F32)
        top_out[rows] = jnp.broadcast_to(top, (128, HD))


def second_half_kernel(q_ref, kv_ref, sum_ref, top_ref, out_ref):
    keys, vals = halves(kv_ref)
    row = lax.broadcasted_iota(jnp.int32, (32, 96), 0)
    col = lax.broadcasted_iota(jnp.int32, (32, 96), 1)
    picks = [(col == (row // 2) * 8 + row % 2 + 6 * s).astype(F32).astype(BF) for s in range(2)]
    edge = jnp.zeros((16, HD), F32)
    done = []

    def finish(n):
        windows = []
        for s in range(2):
            half = slice(64 * s, 64 * s + 64)
            before = done[n - 1][half][48:64] if n > 0 else edge
            after = done[n + 1][half][0:16] if n < 7 else edge
            windows.append(jnp.concatenate([before, done[n][half], after], axis=0))
        for s in range(2):
            near = jnp.dot(picks[s], windows[1 - s].astype(BF), preferred_element_type=F32)
            out_ref[slot(n, s)] = jnp.concatenate([windows[s], near[0:24]], axis=0).astype(BF)

    for n in range(8):
        rows = slice(128 * n, 128 * n + 128)
        scores, top = scores_of(queries_of(q_ref, n), keys)
        before = top_ref[rows, 0:1]
        top = jnp.maximum(top, before)
        weights = jnp.exp2((scores - top) * SCALE).astype(BF)
        kept = jnp.exp2((before - top) * SCALE)
        both = sum_ref[rows] * kept + jnp.dot(weights, vals, preferred_element_type=F32)
        done.append(both[:, 0:HD] / both[:, HD : 2 * HD])
        if n > 0:
            finish(n - 1)
    finish(7)


def project_kernel(a_ref, w_ref, out_ref):
    for x in range(2):
        rows = jnp.concatenate([a_ref[slot(h, x)] for h in range(H)], axis=1)
        projected = jnp.dot(rows, w_ref[...], preferred_element_type=F32)
        scale = lax.rsqrt(jnp.mean(projected * projected, axis=1, keepdims=True) + 1e-06)
        out_ref[x] = (projected * scale).astype(BF)


def laid_out(normed):
    seq = lax.axis_index("seq")
    row = lax.broadcasted_iota(jnp.int32, (12, 8, 256), 1)
    slabs = []
    for x in range(2):
        rows = normed[x].astype(F32)
        middle = pltpu.roll(rows[0:96].reshape(12, 8, 256), 2, 1)
        near = rows[96:120].reshape(3, 8, 256)
        ends = [pltpu.roll(near, 8 - 2 * k, 1) if k else near for k in range(4)]
        ends = jnp.stack(ends, axis=1).reshape(12, 8, 256)
        upper = jnp.where(row < 2, jnp.where(seq == 1, ends, 0.0), middle)
        lower = jnp.where((row < 4) & (seq == 0), pltpu.roll(ends, 2, 1), 0.0)
        lower = jnp.where(row < 2, middle, lower)
        slabs.append(jnp.concatenate([upper, lower], axis=1).reshape(192, 256).astype(BF))
    return slabs


def merge_kernel(w_ref, out_ref):
    def both(parts):
        return ((parts[0], parts[1] + parts[2]), (parts[0] + parts[1], parts[2]))

    taps = [[[w_ref[9 * a + 3 * b + c].astype(F32) for c in range(3)] for b in range(3)] for a in range(3)]
    on_z = [[[m for p in both(taps[a][b]) for m in p] for b in range(3)] for a in range(3)]
    for n in range(4):
        on_y = [both([on_z[a][b][n] for b in range(3)]) for a in range(3)]
        for py in range(2):
            for b in range(2):
                on_x = both([on_y[a][py][b] for a in range(3)])
                for px in range(2):
                    for a in range(2):
                        rows = (2 * a + b) * 128
                        out_ref[2 * px + py, rows : rows + 128, n * 128 : (n + 1) * 128] = on_x[px][a].astype(BF)


def shifted(x, by):
    return pltpu.roll(x, by % x.shape[0], 0)


def x_tile():
    return 2 * lax.axis_index("z") + lax.axis_index("core")


def taps(w1_ref, a, b):
    t = 9 * a + 3 * b
    return jnp.concatenate([w1_ref[t], w1_ref[t + 1], w1_ref[t + 2]], axis=1)


def own_conv_kernel(own_ref, w1_ref, out_ref):
    slabs = laid_out(own_ref[...])
    for x in range(4):
        total = jnp.zeros((160, 384), F32)
        for a in range(3):
            if 2 <= x + a < 4:
                for b in range(3):
                    part = slabs[x + a - 2][16 * b : 16 * b + 160]
                    total = total + jnp.dot(part, taps(w1_ref, a, b), preferred_element_type=F32)
        out_ref[x] = total


def side(at_left, slabs, own_ref, w1_ref):
    gx, gy, seq = x_tile(), 2 * lax.axis_index("chip_x") + lax.axis_index("low_y"), lax.axis_index("seq")
    row = lax.broadcasted_iota(jnp.int32, (160, 128), 0)
    at_z = seq * 8 - 1 + row % 16
    at_y = gy * 8 - 1 + row // 16
    inside = (at_y >= 0) & (at_y < 64) & (at_z >= 0) & (at_z < 16)
    first_tap = jnp.where(at_left, 0, 1)
    outer = [(slabs[0], first_tap), (slabs[1], first_tap + 1)]
    inner = [(jnp.where(at_left, slabs[1], slabs[0]), jnp.where(at_left, 0, 2))]
    results = []
    for x, terms in ((jnp.where(at_left, 0, 3), outer), (jnp.where(at_left, 1, 2), inner)):
        total = own_ref[x]
        for slab, a in terms:
            for b in range(3):
                total = total + jnp.dot(slab[16 * b : 16 * b + 160], taps(w1_ref, a, b), preferred_element_type=F32)
        first = total[:, 0:128] + shifted(total[:, 128:256], -1) + shifted(total[:, 256:384], -2)
        value = first / (1.0 + jnp.exp(-first))
        at_x = gx * 2 - 1 + x
        results.append((x, jnp.where(inside & (at_x >= 0) & (at_x < 32), value, 0.0).astype(BF)))
    return results


def near_conv_kernel(near_ref, own_ref, w1_ref, out_ref):
    at_left = lax.axis_index("core") == 1
    slabs = laid_out(near_ref[...])
    for n, (_, rows) in enumerate(side(at_left, slabs, own_ref, w1_ref)):
        out_ref[n] = rows


def conv_kernel(own_ref, done_ref, far_ref, w1_ref, w2_ref, out_hbm, hidden, field, ready, sems):
    gx = x_tile()
    at_left = lax.axis_index("core") == 0
    there = jnp.where(at_left, gx > 0, gx < 15)
    slabs = [jnp.where(there, slab, jnp.zeros_like(slab)) for slab in laid_out(far_ref[...])]
    hidden[jnp.where(at_left, 3, 0)] = done_ref[0]
    hidden[jnp.where(at_left, 2, 1)] = done_ref[1]
    for x, rows in side(at_left, slabs, own_ref, w1_ref):
        hidden[x] = rows
    copies = []
    for px in range(2):
        for py in range(2):
            rows = [
                [hidden[i + px + a, 16 * (py + b) : 16 * (py + b) + 128] for a in range(2) for b in range(2)]
                for i in range(2)
            ]
            rows = jnp.concatenate([jnp.concatenate(parts, axis=1) for parts in rows], axis=0)
            parts = jnp.dot(rows, w2_ref[2 * px + py], preferred_element_type=F32)
            even = parts[:, 0:128] + shifted(parts[:, 128:256], -1)
            odd = shifted(parts[:, 256:384], -1) + shifted(parts[:, 384:512], -2)
            for pz, part in ((0, even), (1, odd)):
                part = part.reshape(2, 8, 16, 128)
                for i in range(2):
                    for j in range(8):
                        field[2 * i + px, 2 * j + py, pl.ds(pz, 8, stride=2), :] = part[i, j, 0:8]
        for x in (px, px + 2):
            ready[x] = field[x].astype(BF)
            copies.append(pltpu.make_async_copy(ready.at[x], out_hbm.at[x], sems.at[x]))
            copies[-1].start()
    for copy in copies:
        copy.wait()


def body(queries, keys, values, w_out, conv_first, conv_second):
    sent = call(
        pack_kernel,
        [(16, 80, HD)],
        [BF],
        [HB] * 3,
        [
            pltpu.VMEM((2, 64, H * HD), BF),
            pltpu.VMEM((8, H * HD), BF),
            pltpu.VMEM((8, H * HD), BF),
            pltpu.SemaphoreType.DMA((3,)),
        ],
    )(*(pltpu.with_memory_space_constraint(a, pltpu.HBM) for a in (queries.reshape(2, 64, H * HD), keys, values)))
    got = lax.all_to_all(sent, ("chip_x", "seq", "low_y"), 0, 0, tiled=True)
    pair = got[:, 64:80].reshape(16, 2, 8, HD).transpose(1, 0, 2, 3).reshape(1, 256, HD)
    own = lax.all_to_all(jnp.broadcast_to(pair, (8, 256, HD)), "z", 0, 0, tiled=True)
    other = lax.ppermute(own, "core", [(0, 1), (1, 0)])
    summed, top = call(first_half_kernel, [(1024, 2 * HD), (1024, HD)], [F32, F32], [VM, VM])(got, own)
    attended = call(second_half_kernel, [(16, 120, HD)], [BF], [VM] * 4)(got, other, summed, top)
    back = lax.all_to_all(attended, ("chip_x", "seq", "low_y"), 0, 0, tiled=True)
    normed = call(project_kernel, [(2, 120, 256)], [BF], [VM, VM])(back, w_out)
    far = lax.ppermute(normed, ("z", "core"), [(i, (i - 1 + 2 * (i % 2)) % 16) for i in range(16)])
    near = lax.ppermute(normed, "core", [(0, 1), (1, 0)])
    w1 = conv_first.reshape(27, 256, 128)
    merged = call(merge_kernel, [(4, 512, 512)], [BF], [VM])(conv_second.reshape(27, 128, 128))
    own_part = call(own_conv_kernel, [(4, 160, 384)], [F32], [VM, VM])(normed, w1)
    done = call(near_conv_kernel, [(2, 160, 128)], [BF], [VM] * 3)(near, own_part, w1)
    scratch = [
        pltpu.VMEM((4, 160, 128), BF),
        pltpu.VMEM((4, 16, 16, 128), F32),
        pltpu.VMEM((4, 16, 16, 128), BF),
        pltpu.SemaphoreType.DMA((4,)),
    ]
    final = call(conv_kernel, [(4, 16, 16, 128)], [BF], [VM] * 5, scratch, HB)
    return final(own_part, done, far, w1, merged)


def solution(mesh):
    cut = Mesh(mesh.devices.reshape(8, 2, 4, 2, 2), ("z", "core", "chip_x", "low_y", "seq"))
    tokens = P(("z", "core", "chip_x", "low_y", "seq"), None)
    voxels = P(("z", "core"), ("chip_x", "low_y"), "seq", None)
    return jax.shard_map(
        body, mesh=cut, in_specs=(voxels, tokens, tokens, P(), P(), P()), out_specs=voxels, check_vma=False
    )
```

```python
import jax
import jax.numpy as jnp
from jax import lax
from jax.experimental import pallas as pl
from jax.experimental.pallas import tpu as pltpu
from jax.sharding import Mesh, PartitionSpec as P

H = 8
HD = 128
BF = jnp.bfloat16
F32 = jnp.float32
VM = pl.BlockSpec(memory_space=pltpu.VMEM)
HB = pl.BlockSpec(memory_space=pltpu.HBM)
SCALE = HD**-0.5 * 1.4426950408889634


def call(kernel, shapes, dtypes, in_specs, scratch=(), out_spec=VM):
    outs = [jax.ShapeDtypeStruct(shape, dtype) for shape, dtype in zip(shapes, dtypes)]
    one = len(outs) == 1
    return pl.pallas_call(
        kernel,
        out_shape=outs[0] if one else outs,
        in_specs=in_specs,
        out_specs=out_spec if one else [VM] * len(outs),
        scratch_shapes=list(scratch),
        compiler_params=pltpu.CompilerParams(vmem_limit_bytes=24 * 1024 * 1024),
        cost_estimate=pl.CostEstimate(flops=10**6, bytes_accessed=10000, transcendentals=0),
    )


def slot(tile, half):
    return 4 * (tile // 2) + 2 * half + tile % 2


def pack_kernel(q_hbm, k_hbm, v_hbm, out_ref, q_ref, k_ref, v_ref, sems):
    copies = [
        pltpu.make_async_copy(src, dst, sems.at[i])
        for i, (src, dst) in enumerate(((q_hbm, q_ref), (k_hbm, k_ref), (v_hbm, v_ref)))
    ]
    for copy in copies:
        copy.start()
    for copy in copies:
        copy.wait()
    for h in range(H):
        cols = slice(h * HD, (h + 1) * HD)
        pair = jnp.concatenate([k_ref[:, cols].astype(F32), v_ref[:, cols].astype(F32)], axis=0).astype(BF)
        for s in range(2):
            out_ref[slot(h, s), 0:64] = q_ref[s, :, cols]
            out_ref[slot(h, s), 64:80] = pair


def halves(ref):
    keys = ref[:, 0:128].reshape(1024, HD)
    return keys, jnp.concatenate([ref[:, 128:256].reshape(1024, HD), jnp.ones((1024, HD), BF)], axis=1)


def scores_of(q, keys):
    scores = lax.dot_general(q, keys, (((1,), (1,)), ((), ())), preferred_element_type=F32)
    return scores, jnp.max(scores, axis=1, keepdims=True)


def queries_of(q_ref, n):
    return jnp.concatenate([q_ref[slot(n, 0), 0:64], q_ref[slot(n, 1), 0:64]], axis=0)


def first_half_kernel(q_ref, kv_ref, sum_out, top_out):
    keys, vals = halves(kv_ref)
    for n in range(8):
        rows = slice(128 * n, 128 * n + 128)
        scores, top = scores_of(queries_of(q_ref, n), keys)
        weights = jnp.exp2((scores - top) * SCALE).astype(BF)
        sum_out[rows] = jnp.dot(weights, vals, preferred_element_type=F32)
        top_out[rows] = jnp.broadcast_to(top, (128, HD))


def second_half_kernel(q_ref, kv_ref, sum_ref, top_ref, out_ref, windows):
    keys, vals = halves(kv_ref)
    edge = jnp.zeros((16, HD), F32)
    for s in range(2):
        windows[slot(0, s), 0:16] = edge
        windows[slot(7, s), 80:96] = edge
    for n in range(8):
        rows = slice(128 * n, 128 * n + 128)
        scores, top = scores_of(queries_of(q_ref, n), keys)
        before = top_ref[rows, 0:1]
        top = jnp.maximum(top, before)
        weights = jnp.exp2((scores - top) * SCALE).astype(BF)
        kept = jnp.exp2((before - top) * SCALE)
        both = sum_ref[rows] * kept + jnp.dot(weights, vals, preferred_element_type=F32)
        done = both[:, 0:HD] / both[:, HD : 2 * HD]
        for s in range(2):
            half = done[64 * s : 64 * s + 64]
            windows[slot(n, s), 16:80] = half
            if n < 7:
                windows[slot(n + 1, s), 0:16] = half[48:64]
            if n > 0:
                windows[slot(n - 1, s), 80:96] = half[0:16]
    row = lax.broadcasted_iota(jnp.int32, (32, 96), 0)
    col = lax.broadcasted_iota(jnp.int32, (32, 96), 1)
    for s in range(2):
        pick = (col == (row // 2) * 8 + row % 2 + 6 * s).astype(F32).astype(BF)
        for n in range(8):
            near = jnp.dot(pick, windows[slot(n, 1 - s)].astype(BF), preferred_element_type=F32)
            out_ref[slot(n, s)] = jnp.concatenate([windows[slot(n, s)], near[0:24]], axis=0).astype(BF)


def project_kernel(a_ref, w_ref, out_ref):
    for x in range(2):
        rows = jnp.concatenate([a_ref[slot(h, x)] for h in range(H)], axis=1)
        projected = jnp.dot(rows, w_ref[...], preferred_element_type=F32)
        scale = lax.rsqrt(jnp.mean(projected * projected, axis=1, keepdims=True) + 1e-06)
        out_ref[x] = (projected * scale).astype(BF)


def laid_out(normed):
    seq = lax.axis_index("seq")
    row = lax.broadcasted_iota(jnp.int32, (12, 8, 256), 1)
    slabs = []
    for x in range(2):
        rows = normed[x].astype(F32)
        middle = pltpu.roll(rows[0:96].reshape(12, 8, 256), 2, 1)
        near = rows[96:120].reshape(3, 8, 256)
        ends = [pltpu.roll(near, 8 - 2 * k, 1) if k else near for k in range(4)]
        ends = jnp.stack(ends, axis=1).reshape(12, 8, 256)
        upper = jnp.where(row < 2, jnp.where(seq == 1, ends, 0.0), middle)
        lower = jnp.where((row < 4) & (seq == 0), pltpu.roll(ends, 2, 1), 0.0)
        lower = jnp.where(row < 2, middle, lower)
        slabs.append(jnp.concatenate([upper, lower], axis=1).reshape(192, 256).astype(BF))
    return slabs


def merge_kernel(w_ref, out_ref):
    def both(parts):
        return ((parts[0], parts[1] + parts[2]), (parts[0] + parts[1], parts[2]))

    taps = [[[w_ref[9 * a + 3 * b + c].astype(F32) for c in range(3)] for b in range(3)] for a in range(3)]
    on_z = [[[m for p in both(taps[a][b]) for m in p] for b in range(3)] for a in range(3)]
    for n in range(4):
        on_y = [both([on_z[a][b][n] for b in range(3)]) for a in range(3)]
        for py in range(2):
            for b in range(2):
                on_x = both([on_y[a][py][b] for a in range(3)])
                for px in range(2):
                    for a in range(2):
                        rows = (2 * a + b) * 128
                        out_ref[2 * px + py, rows : rows + 128, n * 128 : (n + 1) * 128] = on_x[px][a].astype(BF)


def shifted(x, by):
    return pltpu.roll(x, by % x.shape[0], 0)


def x_tile():
    return 2 * lax.axis_index("z") + lax.axis_index("core")


def taps(w1_ref, a, b):
    t = 9 * a + 3 * b
    return jnp.concatenate([w1_ref[t], w1_ref[t + 1], w1_ref[t + 2]], axis=1)


def own_conv_kernel(own_ref, w1_ref, out_ref):
    slabs = laid_out(own_ref[...])
    for x in range(4):
        total = jnp.zeros((160, 384), F32)
        for a in range(3):
            if 2 <= x + a < 4:
                for b in range(3):
                    part = slabs[x + a - 2][16 * b : 16 * b + 160]
                    total = total + jnp.dot(part, taps(w1_ref, a, b), preferred_element_type=F32)
        out_ref[x] = total


def side(at_left, slabs, own_ref, w1_ref):
    gx, gy, seq = x_tile(), 2 * lax.axis_index("chip_x") + lax.axis_index("low_y"), lax.axis_index("seq")
    row = lax.broadcasted_iota(jnp.int32, (160, 128), 0)
    at_z = seq * 8 - 1 + row % 16
    at_y = gy * 8 - 1 + row // 16
    inside = (at_y >= 0) & (at_y < 64) & (at_z >= 0) & (at_z < 16)
    first_tap = jnp.where(at_left, 0, 1)
    outer = [(slabs[0], first_tap), (slabs[1], first_tap + 1)]
    inner = [(jnp.where(at_left, slabs[1], slabs[0]), jnp.where(at_left, 0, 2))]
    results = []
    for x, terms in ((jnp.where(at_left, 0, 3), outer), (jnp.where(at_left, 1, 2), inner)):
        total = own_ref[x]
        for slab, a in terms:
            for b in range(3):
                total = total + jnp.dot(slab[16 * b : 16 * b + 160], taps(w1_ref, a, b), preferred_element_type=F32)
        first = total[:, 0:128] + shifted(total[:, 128:256], -1) + shifted(total[:, 256:384], -2)
        value = first / (1.0 + jnp.exp(-first))
        at_x = gx * 2 - 1 + x
        results.append((x, jnp.where(inside & (at_x >= 0) & (at_x < 32), value, 0.0).astype(BF)))
    return results


def near_conv_kernel(near_ref, own_ref, w1_ref, out_ref):
    at_left = lax.axis_index("core") == 1
    slabs = laid_out(near_ref[...])
    for n, (_, rows) in enumerate(side(at_left, slabs, own_ref, w1_ref)):
        out_ref[n] = rows


def conv_kernel(own_ref, done_ref, far_ref, w1_ref, w2_ref, out_hbm, hidden, field, ready, sems):
    gx = x_tile()
    at_left = lax.axis_index("core") == 0
    there = jnp.where(at_left, gx > 0, gx < 15)
    slabs = [jnp.where(there, slab, jnp.zeros_like(slab)) for slab in laid_out(far_ref[...])]
    hidden[jnp.where(at_left, 3, 0)] = done_ref[0]
    hidden[jnp.where(at_left, 2, 1)] = done_ref[1]
    for x, rows in side(at_left, slabs, own_ref, w1_ref):
        hidden[x] = rows
    copies = []
    for px in range(2):
        for py in range(2):
            rows = [
                [hidden[i + px + a, 16 * (py + b) : 16 * (py + b) + 128] for a in range(2) for b in range(2)]
                for i in range(2)
            ]
            rows = jnp.concatenate([jnp.concatenate(parts, axis=1) for parts in rows], axis=0)
            parts = jnp.dot(rows, w2_ref[2 * px + py], preferred_element_type=F32)
            even = parts[:, 0:128] + shifted(parts[:, 128:256], -1)
            odd = shifted(parts[:, 256:384], -1) + shifted(parts[:, 384:512], -2)
            for pz, part in ((0, even), (1, odd)):
                part = part.reshape(2, 8, 16, 128)
                for i in range(2):
                    for j in range(8):
                        field[2 * i + px, 2 * j + py, pl.ds(pz, 8, stride=2), :] = part[i, j, 0:8]
        for x in (px, px + 2):
            ready[x] = field[x].astype(BF)
            copies.append(pltpu.make_async_copy(ready.at[x], out_hbm.at[x], sems.at[x]))
            copies[-1].start()
    for copy in copies:
        copy.wait()


def body(queries, keys, values, w_out, conv_first, conv_second):
    sent = call(
        pack_kernel,
        [(16, 80, HD)],
        [BF],
        [HB] * 3,
        [
            pltpu.VMEM((2, 64, H * HD), BF),
            pltpu.VMEM((8, H * HD), BF),
            pltpu.VMEM((8, H * HD), BF),
            pltpu.SemaphoreType.DMA((3,)),
        ],
    )(*(pltpu.with_memory_space_constraint(a, pltpu.HBM) for a in (queries.reshape(2, 64, H * HD), keys, values)))
    got = lax.all_to_all(sent, ("chip_x", "seq", "low_y"), 0, 0, tiled=True)
    pair = got[:, 64:80].reshape(16, 2, 8, HD).transpose(1, 0, 2, 3).reshape(1, 256, HD)
    own = lax.all_to_all(jnp.broadcast_to(pair, (8, 256, HD)), "z", 0, 0, tiled=True)
    other = lax.ppermute(own, "core", [(0, 1), (1, 0)])
    summed, top = call(first_half_kernel, [(1024, 2 * HD), (1024, HD)], [F32, F32], [VM, VM])(got, own)
    attended = call(second_half_kernel, [(16, 120, HD)], [BF], [VM] * 4, [pltpu.VMEM((16, 96, HD), F32)])(got, other, summed, top)
    back = lax.all_to_all(attended, ("chip_x", "seq", "low_y"), 0, 0, tiled=True)
    normed = call(project_kernel, [(2, 120, 256)], [BF], [VM, VM])(back, w_out)
    far = lax.ppermute(normed, ("z", "core"), [(i, (i - 1 + 2 * (i % 2)) % 16) for i in range(16)])
    near = lax.ppermute(normed, "core", [(0, 1), (1, 0)])
    w1 = conv_first.reshape(27, 256, 128)
    merged = call(merge_kernel, [(4, 512, 512)], [BF], [VM])(conv_second.reshape(27, 128, 128))
    own_part = call(own_conv_kernel, [(4, 160, 384)], [F32], [VM, VM])(normed, w1)
    done = call(near_conv_kernel, [(2, 160, 128)], [BF], [VM] * 3)(near, own_part, w1)
    scratch = [
        pltpu.VMEM((4, 160, 128), BF),
        pltpu.VMEM((4, 16, 16, 128), F32),
        pltpu.VMEM((4, 16, 16, 128), BF),
        pltpu.SemaphoreType.DMA((4,)),
    ]
    final = call(conv_kernel, [(4, 16, 16, 128)], [BF], [VM] * 5, scratch, HB)
    return final(own_part, done, far, w1, merged)


def solution(mesh):
    cut = Mesh(mesh.devices.reshape(8, 2, 4, 2, 2), ("z", "core", "chip_x", "low_y", "seq"))
    tokens = P(("z", "core", "chip_x", "low_y", "seq"), None)
    voxels = P(("z", "core"), ("chip_x", "low_y"), "seq", None)
    return jax.shard_map(
        body, mesh=cut, in_specs=(voxels, tokens, tokens, P(), P(), P()), out_specs=voxels, check_vma=False
    )
```

```python
import jax
import jax.numpy as jnp
from jax import lax
from jax.experimental import pallas as pl
from jax.experimental.pallas import tpu as pltpu
from jax.sharding import Mesh, PartitionSpec as P

H = 8
HD = 128
BF = jnp.bfloat16
F32 = jnp.float32
VM = pl.BlockSpec(memory_space=pltpu.VMEM)
HB = pl.BlockSpec(memory_space=pltpu.HBM)
SCALE = HD**-0.5 * 1.4426950408889634


def call(kernel, shapes, dtypes, in_specs, scratch=(), out_spec=VM):
    outs = [jax.ShapeDtypeStruct(shape, dtype) for shape, dtype in zip(shapes, dtypes)]
    one = len(outs) == 1
    return pl.pallas_call(
        kernel,
        out_shape=outs[0] if one else outs,
        in_specs=in_specs,
        out_specs=out_spec if one else [VM] * len(outs),
        scratch_shapes=list(scratch),
        compiler_params=pltpu.CompilerParams(vmem_limit_bytes=24 * 1024 * 1024),
        cost_estimate=pl.CostEstimate(flops=10**6, bytes_accessed=10000, transcendentals=0),
    )


def slot(tile, half):
    return 4 * (tile // 2) + 2 * half + tile % 2


def spread_kernel(q_hbm, k_hbm, v_hbm, out_ref, q_ref, k_ref, v_ref, sems):
    copies = [
        pltpu.make_async_copy(src, dst, sems.at[i])
        for i, (src, dst) in enumerate(((k_hbm, k_ref), (v_hbm, v_ref), (q_hbm, q_ref)))
    ]
    for copy in copies:
        copy.start()
    for copy in copies[0:2]:
        copy.wait()
    pair = jnp.concatenate([k_ref[...].astype(F32), v_ref[...].astype(F32)], axis=0).astype(BF)
    for z in range(8):
        out_ref[z] = pair
    copies[2].wait()


def pack_kernel(q_ref, kv_ref, out_ref):
    for h in range(H):
        cols = slice(h * HD, (h + 1) * HD)
        pairs = [kv_ref[z, :, cols].astype(F32) for z in range(8)]
        keys = jnp.concatenate([pair[0:8] for pair in pairs], axis=0).astype(BF)
        vals = jnp.concatenate([pair[8:16] for pair in pairs], axis=0).astype(BF)
        for s in range(2):
            out_ref[slot(h, s), 0:64] = q_ref[s, :, cols]
            out_ref[slot(h, s), 64:128] = keys
            out_ref[slot(h, s), 128:192] = vals


def halves(ref):
    keys = ref[:, 64:128].reshape(1024, HD)
    return keys, jnp.concatenate([ref[:, 128:192].reshape(1024, HD), jnp.ones((1024, HD), BF)], axis=1)


def scores_of(q, keys):
    scores = lax.dot_general(q, keys, (((1,), (1,)), ((), ())), preferred_element_type=F32)
    return scores, jnp.max(scores, axis=1, keepdims=True)


def queries_of(q_ref, n):
    return jnp.concatenate([q_ref[slot(n, 0), 0:64], q_ref[slot(n, 1), 0:64]], axis=0)


def first_half_kernel(q_ref, sum_out, top_out):
    keys, vals = halves(q_ref)
    for n in range(8):
        rows = slice(128 * n, 128 * n + 128)
        scores, top = scores_of(queries_of(q_ref, n), keys)
        weights = jnp.exp2((scores - top) * SCALE).astype(BF)
        sum_out[rows] = jnp.dot(weights, vals, preferred_element_type=F32)
        top_out[rows] = jnp.broadcast_to(top, (128, HD))


def second_half_kernel(q_ref, kv_ref, sum_ref, top_ref, out_ref, windows):
    keys, vals = halves(kv_ref)
    edge = jnp.zeros((16, HD), F32)
    for s in range(2):
        windows[slot(0, s), 0:16] = edge
        windows[slot(7, s), 80:96] = edge
    for n in range(8):
        rows = slice(128 * n, 128 * n + 128)
        scores, top = scores_of(queries_of(q_ref, n), keys)
        before = top_ref[rows, 0:1]
        top = jnp.maximum(top, before)
        weights = jnp.exp2((scores - top) * SCALE).astype(BF)
        kept = jnp.exp2((before - top) * SCALE)
        both = sum_ref[rows] * kept + jnp.dot(weights, vals, preferred_element_type=F32)
        done = both[:, 0:HD] / both[:, HD : 2 * HD]
        for s in range(2):
            half = done[64 * s : 64 * s + 64]
            windows[slot(n, s), 16:80] = half
            if n < 7:
                windows[slot(n + 1, s), 0:16] = half[48:64]
            if n > 0:
                windows[slot(n - 1, s), 80:96] = half[0:16]
    row = lax.broadcasted_iota(jnp.int32, (32, 96), 0)
    col = lax.broadcasted_iota(jnp.int32, (32, 96), 1)
    for s in range(2):
        pick = (col == (row // 2) * 8 + row % 2 + 6 * s).astype(F32).astype(BF)
        for n in range(8):
            near = jnp.dot(pick, windows[slot(n, 1 - s)].astype(BF), preferred_element_type=F32)
            out_ref[slot(n, s)] = jnp.concatenate([windows[slot(n, s)], near[0:24]], axis=0).astype(BF)


def project_kernel(a_ref, w_ref, out_ref):
    for x in range(2):
        rows = jnp.concatenate([a_ref[slot(h, x)] for h in range(H)], axis=1)
        projected = jnp.dot(rows, w_ref[...], preferred_element_type=F32)
        scale = lax.rsqrt(jnp.mean(projected * projected, axis=1, keepdims=True) + 1e-06)
        out_ref[x] = (projected * scale).astype(BF)


def laid_out(normed):
    seq = lax.axis_index("seq")
    row = lax.broadcasted_iota(jnp.int32, (12, 8, 256), 1)
    slabs = []
    for x in range(2):
        rows = normed[x].astype(F32)
        middle = pltpu.roll(rows[0:96].reshape(12, 8, 256), 2, 1)
        near = rows[96:120].reshape(3, 8, 256)
        ends = [pltpu.roll(near, 8 - 2 * k, 1) if k else near for k in range(4)]
        ends = jnp.stack(ends, axis=1).reshape(12, 8, 256)
        upper = jnp.where(row < 2, jnp.where(seq == 1, ends, 0.0), middle)
        lower = jnp.where((row < 4) & (seq == 0), pltpu.roll(ends, 2, 1), 0.0)
        lower = jnp.where(row < 2, middle, lower)
        slabs.append(jnp.concatenate([upper, lower], axis=1).reshape(192, 256).astype(BF))
    return slabs


def merge_kernel(w_ref, out_ref):
    def both(parts):
        return ((parts[0], parts[1] + parts[2]), (parts[0] + parts[1], parts[2]))

    taps = [[[w_ref[9 * a + 3 * b + c].astype(F32) for c in range(3)] for b in range(3)] for a in range(3)]
    on_z = [[[m for p in both(taps[a][b]) for m in p] for b in range(3)] for a in range(3)]
    for n in range(4):
        on_y = [both([on_z[a][b][n] for b in range(3)]) for a in range(3)]
        for py in range(2):
            for b in range(2):
                on_x = both([on_y[a][py][b] for a in range(3)])
                for px in range(2):
                    for a in range(2):
                        rows = (2 * a + b) * 128
                        out_ref[2 * px + py, rows : rows + 128, n * 128 : (n + 1) * 128] = on_x[px][a].astype(BF)


def shifted(x, by):
    return pltpu.roll(x, by % x.shape[0], 0)


def x_tile():
    return 2 * lax.axis_index("z") + lax.axis_index("core")


def taps(w1_ref, a, b):
    t = 9 * a + 3 * b
    return jnp.concatenate([w1_ref[t], w1_ref[t + 1], w1_ref[t + 2]], axis=1)


def own_conv_kernel(own_ref, w1_ref, out_ref):
    slabs = laid_out(own_ref[...])
    for x in range(4):
        total = jnp.zeros((160, 384), F32)
        for a in range(3):
            if 2 <= x + a < 4:
                for b in range(3):
                    part = slabs[x + a - 2][16 * b : 16 * b + 160]
                    total = total + jnp.dot(part, taps(w1_ref, a, b), preferred_element_type=F32)
        out_ref[x] = total


def side(at_left, slabs, own_ref, w1_ref):
    gx, gy, seq = x_tile(), 2 * lax.axis_index("chip_x") + lax.axis_index("low_y"), lax.axis_index("seq")
    row = lax.broadcasted_iota(jnp.int32, (160, 128), 0)
    at_z = seq * 8 - 1 + row % 16
    at_y = gy * 8 - 1 + row // 16
    inside = (at_y >= 0) & (at_y < 64) & (at_z >= 0) & (at_z < 16)
    first_tap = jnp.where(at_left, 0, 1)
    outer = [(slabs[0], first_tap), (slabs[1], first_tap + 1)]
    inner = [(jnp.where(at_left, slabs[1], slabs[0]), jnp.where(at_left, 0, 2))]
    results = []
    for x, terms in ((jnp.where(at_left, 0, 3), outer), (jnp.where(at_left, 1, 2), inner)):
        total = own_ref[x]
        for slab, a in terms:
            for b in range(3):
                total = total + jnp.dot(slab[16 * b : 16 * b + 160], taps(w1_ref, a, b), preferred_element_type=F32)
        first = total[:, 0:128] + shifted(total[:, 128:256], -1) + shifted(total[:, 256:384], -2)
        value = first / (1.0 + jnp.exp(-first))
        at_x = gx * 2 - 1 + x
        results.append((x, jnp.where(inside & (at_x >= 0) & (at_x < 32), value, 0.0).astype(BF)))
    return results


def near_conv_kernel(near_ref, own_ref, w1_ref, out_ref):
    at_left = lax.axis_index("core") == 1
    slabs = laid_out(near_ref[...])
    for n, (_, rows) in enumerate(side(at_left, slabs, own_ref, w1_ref)):
        out_ref[n] = rows


def conv_kernel(own_ref, done_ref, far_ref, w1_ref, w2_ref, out_hbm, hidden, field, ready, sems):
    gx = x_tile()
    at_left = lax.axis_index("core") == 0
    there = jnp.where(at_left, gx > 0, gx < 15)
    slabs = [jnp.where(there, slab, jnp.zeros_like(slab)) for slab in laid_out(far_ref[...])]
    hidden[jnp.where(at_left, 3, 0)] = done_ref[0]
    hidden[jnp.where(at_left, 2, 1)] = done_ref[1]
    for x, rows in side(at_left, slabs, own_ref, w1_ref):
        hidden[x] = rows
    copies = []
    for px in range(2):
        for py in range(2):
            rows = [
                [hidden[i + px + a, 16 * (py + b) : 16 * (py + b) + 128] for a in range(2) for b in range(2)]
                for i in range(2)
            ]
            rows = jnp.concatenate([jnp.concatenate(parts, axis=1) for parts in rows], axis=0)
            parts = jnp.dot(rows, w2_ref[2 * px + py], preferred_element_type=F32)
            even = parts[:, 0:128] + shifted(parts[:, 128:256], -1)
            odd = shifted(parts[:, 256:384], -1) + shifted(parts[:, 384:512], -2)
            for pz, part in ((0, even), (1, odd)):
                part = part.reshape(2, 8, 16, 128)
                for i in range(2):
                    for j in range(8):
                        field[2 * i + px, 2 * j + py, pl.ds(pz, 8, stride=2), :] = part[i, j, 0:8]
        for x in (px, px + 2):
            ready[x] = field[x].astype(BF)
            copies.append(pltpu.make_async_copy(ready.at[x], out_hbm.at[x], sems.at[x]))
            copies[-1].start()
    for copy in copies:
        copy.wait()


def body(queries, keys, values, w_out, conv_first, conv_second):
    rows = queries.reshape(2, 64, H * HD)
    in_hbm = [pltpu.with_memory_space_constraint(array, pltpu.HBM) for array in (rows, keys, values)]
    scratch = [pltpu.VMEM((8, H * HD), BF), pltpu.VMEM((8, H * HD), BF), pltpu.SemaphoreType.DMA((3,))]
    spread, rows = call(spread_kernel, [(8, 16, H * HD), rows.shape], [BF, BF], [HB] * 3, scratch)(*in_hbm)
    tokens = lax.all_to_all(spread, "z", 0, 0, tiled=True)
    sent = call(pack_kernel, [(16, 192, HD)], [BF], [VM] * 2)(rows, tokens)
    got = lax.all_to_all(sent, ("chip_x", "seq", "low_y"), 0, 0, tiled=True)
    other = lax.ppermute(got, "core", [(0, 1), (1, 0)])
    summed, top = call(first_half_kernel, [(1024, 2 * HD), (1024, HD)], [F32, F32], [VM])(got)
    attended = call(second_half_kernel, [(16, 120, HD)], [BF], [VM] * 4, [pltpu.VMEM((16, 96, HD), F32)])(got, other, summed, top)
    back = lax.all_to_all(attended, ("chip_x", "seq", "low_y"), 0, 0, tiled=True)
    normed = call(project_kernel, [(2, 120, 256)], [BF], [VM, VM])(back, w_out)
    far = lax.ppermute(normed, ("z", "core"), [(i, (i - 1 + 2 * (i % 2)) % 16) for i in range(16)])
    near = lax.ppermute(normed, "core", [(0, 1), (1, 0)])
    w1 = conv_first.reshape(27, 256, 128)
    merged = call(merge_kernel, [(4, 512, 512)], [BF], [VM])(conv_second.reshape(27, 128, 128))
    own_part = call(own_conv_kernel, [(4, 160, 384)], [F32], [VM, VM])(normed, w1)
    done = call(near_conv_kernel, [(2, 160, 128)], [BF], [VM] * 3)(near, own_part, w1)
    scratch = [
        pltpu.VMEM((4, 160, 128), BF),
        pltpu.VMEM((4, 16, 16, 128), F32),
        pltpu.VMEM((4, 16, 16, 128), BF),
        pltpu.SemaphoreType.DMA((4,)),
    ]
    final = call(conv_kernel, [(4, 16, 16, 128)], [BF], [VM] * 5, scratch, HB)
    return final(own_part, done, far, w1, merged)


def solution(mesh):
    cut = Mesh(mesh.devices.reshape(8, 2, 4, 2, 2), ("z", "core", "chip_x", "low_y", "seq"))
    tokens = P(("z", "core", "chip_x", "low_y", "seq"), None)
    voxels = P(("z", "core"), ("chip_x", "low_y"), "seq", None)
    return jax.shard_map(
        body, mesh=cut, in_specs=(voxels, tokens, tokens, P(), P(), P()), out_specs=voxels, check_vma=False
    )
```

```python
import jax
import jax.numpy as jnp
from jax import lax
from jax.experimental import pallas as pl
from jax.experimental.pallas import tpu as pltpu
from jax.sharding import Mesh, PartitionSpec as P

H = 8
HD = 128
BF = jnp.bfloat16
F32 = jnp.float32
VM = pl.BlockSpec(memory_space=pltpu.VMEM)
HB = pl.BlockSpec(memory_space=pltpu.HBM)
SCALE = HD**-0.5 * 1.4426950408889634


def call(kernel, shapes, dtypes, in_specs, scratch=(), out_spec=VM):
    outs = [jax.ShapeDtypeStruct(shape, dtype) for shape, dtype in zip(shapes, dtypes)]
    one = len(outs) == 1
    return pl.pallas_call(
        kernel,
        out_shape=outs[0] if one else outs,
        in_specs=in_specs,
        out_specs=out_spec if one else [VM] * len(outs),
        scratch_shapes=list(scratch),
        compiler_params=pltpu.CompilerParams(vmem_limit_bytes=24 * 1024 * 1024),
        cost_estimate=pl.CostEstimate(flops=10**6, bytes_accessed=10000, transcendentals=0),
    )


def slot(tile, half):
    return 8 * half + 4 * (tile % 2) + tile // 2


def spread_kernel(q_hbm, k_hbm, v_hbm, out_ref, q_ref, k_ref, v_ref, sems):
    copies = [
        pltpu.make_async_copy(src, dst, sems.at[i])
        for i, (src, dst) in enumerate(((k_hbm, k_ref), (v_hbm, v_ref), (q_hbm, q_ref)))
    ]
    for copy in copies:
        copy.start()
    for copy in copies[0:2]:
        copy.wait()
    pair = jnp.concatenate([k_ref[...].astype(F32), v_ref[...].astype(F32)], axis=0).astype(BF)
    for z in range(8):
        out_ref[z] = pair
    copies[2].wait()


def pack_kernel(q_ref, kv_ref, out_ref):
    for h in range(H):
        cols = slice(h * HD, (h + 1) * HD)
        pairs = [kv_ref[z, :, cols].astype(F32) for z in range(8)]
        keys = jnp.concatenate([pair[0:8] for pair in pairs], axis=0).astype(BF)
        vals = jnp.concatenate([pair[8:16] for pair in pairs], axis=0).astype(BF)
        for s in range(2):
            out_ref[slot(h, s), 0:64] = q_ref[s, :, cols]
            out_ref[slot(h, s), 64:128] = keys
            out_ref[slot(h, s), 128:192] = vals


def halves(ref, at):
    keys = ref[:, at : at + 64].reshape(1024, HD)
    return keys, jnp.concatenate([ref[:, at + 64 : at + 128].reshape(1024, HD), jnp.ones((1024, HD), BF)], axis=1)


def scores_of(q, keys):
    scores = lax.dot_general(q, keys, (((1,), (1,)), ((), ())), preferred_element_type=F32)
    return scores, jnp.max(scores, axis=1, keepdims=True)


def queries_of(q_ref, n):
    return jnp.concatenate([q_ref[slot(n, 0), 0:64], q_ref[slot(n, 1), 0:64]], axis=0)


def first_half_kernel(q_ref, sum_out, top_out):
    keys, vals = halves(q_ref, 64)
    for n in range(8):
        rows = slice(128 * n, 128 * n + 128)
        scores, top = scores_of(queries_of(q_ref, n), keys)
        weights = jnp.exp2((scores - top) * SCALE).astype(BF)
        sum_out[rows] = jnp.dot(weights, vals, preferred_element_type=F32)
        top_out[rows] = jnp.broadcast_to(top, (128, HD))


def second_half_kernel(q_ref, kv_ref, sum_ref, top_ref, out_ref, windows):
    keys, vals = halves(kv_ref, 0)
    edge = jnp.zeros((16, HD), F32)
    for s in range(2):
        windows[slot(0, s), 0:16] = edge
        windows[slot(7, s), 80:96] = edge
    for n in range(8):
        rows = slice(128 * n, 128 * n + 128)
        scores, top = scores_of(queries_of(q_ref, n), keys)
        before = top_ref[rows, 0:1]
        top = jnp.maximum(top, before)
        weights = jnp.exp2((scores - top) * SCALE).astype(BF)
        kept = jnp.exp2((before - top) * SCALE)
        both = sum_ref[rows] * kept + jnp.dot(weights, vals, preferred_element_type=F32)
        done = both[:, 0:HD] / both[:, HD : 2 * HD]
        for s in range(2):
            half = done[64 * s : 64 * s + 64]
            windows[slot(n, s), 16:80] = half
            if n < 7:
                windows[slot(n + 1, s), 0:16] = half[48:64]
            if n > 0:
                windows[slot(n - 1, s), 80:96] = half[0:16]
    row = lax.broadcasted_iota(jnp.int32, (32, 96), 0)
    col = lax.broadcasted_iota(jnp.int32, (32, 96), 1)
    for s in range(2):
        pick = (col == (row // 2) * 8 + row % 2 + 6 * s).astype(F32).astype(BF)
        for n in range(8):
            near = jnp.dot(pick, windows[slot(n, 1 - s)].astype(BF), preferred_element_type=F32)
            out_ref[slot(n, s)] = jnp.concatenate([windows[slot(n, s)], near[0:24]], axis=0).astype(BF)


def project_kernel(a_ref, w_ref, out_ref):
    for x in range(2):
        rows = jnp.concatenate([a_ref[slot(h, x)] for h in range(H)], axis=1)
        projected = jnp.dot(rows, w_ref[...], preferred_element_type=F32)
        scale = lax.rsqrt(jnp.mean(projected * projected, axis=1, keepdims=True) + 1e-06)
        out_ref[x] = (projected * scale).astype(BF)


def laid_out(normed):
    seq = lax.axis_index("seq")
    row = lax.broadcasted_iota(jnp.int32, (12, 8, 256), 1)
    slabs = []
    for x in range(2):
        rows = normed[x].astype(F32)
        middle = pltpu.roll(rows[0:96].reshape(12, 8, 256), 2, 1)
        near = rows[96:120].reshape(3, 8, 256)
        ends = [pltpu.roll(near, 8 - 2 * k, 1) if k else near for k in range(4)]
        ends = jnp.stack(ends, axis=1).reshape(12, 8, 256)
        upper = jnp.where(row < 2, jnp.where(seq == 1, ends, 0.0), middle)
        lower = jnp.where((row < 4) & (seq == 0), pltpu.roll(ends, 2, 1), 0.0)
        lower = jnp.where(row < 2, middle, lower)
        slabs.append(jnp.concatenate([upper, lower], axis=1).reshape(192, 256).astype(BF))
    return slabs


def merge_kernel(w_ref, out_ref):
    def both(parts):
        return ((parts[0], parts[1] + parts[2]), (parts[0] + parts[1], parts[2]))

    taps = [[[w_ref[9 * a + 3 * b + c].astype(F32) for c in range(3)] for b in range(3)] for a in range(3)]
    on_z = [[[m for p in both(taps[a][b]) for m in p] for b in range(3)] for a in range(3)]
    for n in range(4):
        on_y = [both([on_z[a][b][n] for b in range(3)]) for a in range(3)]
        for py in range(2):
            for b in range(2):
                on_x = both([on_y[a][py][b] for a in range(3)])
                for px in range(2):
                    for a in range(2):
                        rows = (2 * a + b) * 128
                        out_ref[2 * px + py, rows : rows + 128, n * 128 : (n + 1) * 128] = on_x[px][a].astype(BF)


def shifted(x, by):
    return pltpu.roll(x, by % x.shape[0], 0)


def x_tile():
    return 2 * lax.axis_index("z") + lax.axis_index("core")


def taps(w1_ref, a, b):
    t = 9 * a + 3 * b
    return jnp.concatenate([w1_ref[t], w1_ref[t + 1], w1_ref[t + 2]], axis=1)


def own_conv_kernel(own_ref, w1_ref, out_ref):
    slabs = laid_out(own_ref[...])
    for x in range(4):
        total = jnp.zeros((160, 384), F32)
        for a in range(3):
            if 2 <= x + a < 4:
                for b in range(3):
                    part = slabs[x + a - 2][16 * b : 16 * b + 160]
                    total = total + jnp.dot(part, taps(w1_ref, a, b), preferred_element_type=F32)
        out_ref[x] = total


def side(at_left, slabs, own_ref, w1_ref):
    gx, gy, seq = x_tile(), 2 * lax.axis_index("chip_x") + lax.axis_index("low_y"), lax.axis_index("seq")
    row = lax.broadcasted_iota(jnp.int32, (160, 128), 0)
    at_z = seq * 8 - 1 + row % 16
    at_y = gy * 8 - 1 + row // 16
    inside = (at_y >= 0) & (at_y < 64) & (at_z >= 0) & (at_z < 16)
    first_tap = jnp.where(at_left, 0, 1)
    outer = [(slabs[0], first_tap), (slabs[1], first_tap + 1)]
    inner = [(jnp.where(at_left, slabs[1], slabs[0]), jnp.where(at_left, 0, 2))]
    results = []
    for x, terms in ((jnp.where(at_left, 0, 3), outer), (jnp.where(at_left, 1, 2), inner)):
        total = own_ref[x]
        for slab, a in terms:
            for b in range(3):
                total = total + jnp.dot(slab[16 * b : 16 * b + 160], taps(w1_ref, a, b), preferred_element_type=F32)
        first = total[:, 0:128] + shifted(total[:, 128:256], -1) + shifted(total[:, 256:384], -2)
        value = first / (1.0 + jnp.exp(-first))
        at_x = gx * 2 - 1 + x
        results.append((x, jnp.where(inside & (at_x >= 0) & (at_x < 32), value, 0.0).astype(BF)))
    return results


def near_conv_kernel(near_ref, own_ref, w1_ref, out_ref):
    at_left = lax.axis_index("core") == 1
    slabs = laid_out(near_ref[...])
    for n, (_, rows) in enumerate(side(at_left, slabs, own_ref, w1_ref)):
        out_ref[n] = rows


def conv_kernel(own_ref, done_ref, far_ref, w1_ref, w2_ref, out_hbm, hidden, field, ready, sems):
    gx = x_tile()
    at_left = lax.axis_index("core") == 0
    there = jnp.where(at_left, gx > 0, gx < 15)
    slabs = [jnp.where(there, slab, jnp.zeros_like(slab)) for slab in laid_out(far_ref[...])]
    hidden[jnp.where(at_left, 3, 0)] = done_ref[0]
    hidden[jnp.where(at_left, 2, 1)] = done_ref[1]
    for x, rows in side(at_left, slabs, own_ref, w1_ref):
        hidden[x] = rows
    copies = []
    for px in range(2):
        for py in range(2):
            rows = [
                [hidden[i + px + a, 16 * (py + b) : 16 * (py + b) + 128] for a in range(2) for b in range(2)]
                for i in range(2)
            ]
            rows = jnp.concatenate([jnp.concatenate(parts, axis=1) for parts in rows], axis=0)
            parts = jnp.dot(rows, w2_ref[2 * px + py], preferred_element_type=F32)
            even = parts[:, 0:128] + shifted(parts[:, 128:256], -1)
            odd = shifted(parts[:, 256:384], -1) + shifted(parts[:, 384:512], -2)
            for pz, part in ((0, even), (1, odd)):
                part = part.reshape(2, 8, 16, 128)
                for i in range(2):
                    for j in range(8):
                        field[2 * i + px, 2 * j + py, pl.ds(pz, 8, stride=2), :] = part[i, j, 0:8]
        for x in (px, px + 2):
            ready[x] = field[x].astype(BF)
            copies.append(pltpu.make_async_copy(ready.at[x], out_hbm.at[x], sems.at[x]))
            copies[-1].start()
    for copy in copies:
        copy.wait()


def body(queries, keys, values, w_out, conv_first, conv_second):
    rows = queries.reshape(2, 64, H * HD)
    in_hbm = [pltpu.with_memory_space_constraint(array, pltpu.HBM) for array in (rows, keys, values)]
    scratch = [pltpu.VMEM((8, H * HD), BF), pltpu.VMEM((8, H * HD), BF), pltpu.SemaphoreType.DMA((3,))]
    spread, rows = call(spread_kernel, [(8, 16, H * HD), rows.shape], [BF, BF], [HB] * 3, scratch)(*in_hbm)
    tokens = lax.all_to_all(spread, "z", 0, 0, tiled=True)
    sent = call(pack_kernel, [(16, 192, HD)], [BF], [VM] * 2)(rows, tokens)
    got = lax.all_to_all(sent, ("seq", "low_y", "chip_x"), 0, 0, tiled=True)
    other = lax.ppermute(got[:, 64:192], "core", [(0, 1), (1, 0)])
    summed, top = call(first_half_kernel, [(1024, 2 * HD), (1024, HD)], [F32, F32], [VM])(got)
    attended = call(second_half_kernel, [(16, 120, HD)], [BF], [VM] * 4, [pltpu.VMEM((16, 96, HD), F32)])(got, other, summed, top)
    back = lax.all_to_all(attended, ("seq", "low_y", "chip_x"), 0, 0, tiled=True)
    normed = call(project_kernel, [(2, 120, 256)], [BF], [VM, VM])(back, w_out)
    far = lax.ppermute(normed, ("z", "core"), [(i, (i - 1 + 2 * (i % 2)) % 16) for i in range(16)])
    near = lax.ppermute(normed, "core", [(0, 1), (1, 0)])
    w1 = conv_first.reshape(27, 256, 128)
    merged = call(merge_kernel, [(4, 512, 512)], [BF], [VM])(conv_second.reshape(27, 128, 128))
    own_part = call(own_conv_kernel, [(4, 160, 384)], [F32], [VM, VM])(normed, w1)
    done = call(near_conv_kernel, [(2, 160, 128)], [BF], [VM] * 3)(near, own_part, w1)
    scratch = [
        pltpu.VMEM((4, 160, 128), BF),
        pltpu.VMEM((4, 16, 16, 128), F32),
        pltpu.VMEM((4, 16, 16, 128), BF),
        pltpu.SemaphoreType.DMA((4,)),
    ]
    final = call(conv_kernel, [(4, 16, 16, 128)], [BF], [VM] * 5, scratch, HB)
    return final(own_part, done, far, w1, merged)


def solution(mesh):
    cut = Mesh(mesh.devices.reshape(8, 2, 4, 2, 2), ("z", "core", "chip_x", "low_y", "seq"))
    tokens = P(("z", "core", "chip_x", "low_y", "seq"), None)
    voxels = P(("z", "core"), ("chip_x", "low_y"), "seq", None)
    return jax.shard_map(
        body, mesh=cut, in_specs=(voxels, tokens, tokens, P(), P(), P()), out_specs=voxels, check_vma=False
    )
```

```python
import jax
import jax.numpy as jnp
from jax import lax
from jax.experimental import pallas as pl
from jax.experimental.pallas import tpu as pltpu
from jax.sharding import Mesh, PartitionSpec as P

H = 8
HD = 128
BF = jnp.bfloat16
F32 = jnp.float32
VM = pl.BlockSpec(memory_space=pltpu.VMEM)
HB = pl.BlockSpec(memory_space=pltpu.HBM)
SCALE = HD**-0.5 * 1.4426950408889634


def call(kernel, shapes, dtypes, in_specs, scratch=(), out_spec=VM):
    outs = [jax.ShapeDtypeStruct(shape, dtype) for shape, dtype in zip(shapes, dtypes)]
    one = len(outs) == 1
    return pl.pallas_call(
        kernel,
        out_shape=outs[0] if one else outs,
        in_specs=in_specs,
        out_specs=out_spec if one else [VM] * len(outs),
        scratch_shapes=list(scratch),
        compiler_params=pltpu.CompilerParams(vmem_limit_bytes=24 * 1024 * 1024),
        cost_estimate=pl.CostEstimate(flops=10**6, bytes_accessed=10000, transcendentals=0),
    )


def slot(tile, half):
    return 8 * half + 4 * (tile % 2) + tile // 2


def spread_kernel(q_hbm, k_hbm, v_hbm, out_ref, q_ref, k_ref, v_ref, sems):
    copies = [
        pltpu.make_async_copy(src, dst, sems.at[i])
        for i, (src, dst) in enumerate(((k_hbm, k_ref), (v_hbm, v_ref), (q_hbm, q_ref)))
    ]
    for copy in copies:
        copy.start()
    for copy in copies[0:2]:
        copy.wait()
    pair = jnp.concatenate([k_ref[...].astype(F32), v_ref[...].astype(F32)], axis=0).astype(BF)
    for z in range(8):
        out_ref[z] = pair
    copies[2].wait()


def pack_kernel(q_ref, kv_ref, out_ref):
    for h in range(H):
        cols = slice(h * HD, (h + 1) * HD)
        pairs = [kv_ref[z, :, cols].astype(F32) for z in range(8)]
        keys = jnp.concatenate([pair[0:8] for pair in pairs], axis=0).astype(BF)
        vals = jnp.concatenate([pair[8:16] for pair in pairs], axis=0).astype(BF)
        for s in range(2):
            out_ref[slot(h, s), 0:64] = q_ref[s, :, cols]
            out_ref[slot(h, s), 64:128] = keys
            out_ref[slot(h, s), 128:192] = vals


def halves(ref, at):
    keys = ref[:, at : at + 64].reshape(1024, HD)
    return keys, jnp.concatenate([ref[:, at + 64 : at + 128].reshape(1024, HD), jnp.ones((1024, HD), BF)], axis=1)


def scores_of(q, keys):
    scores = lax.dot_general(q, keys, (((1,), (1,)), ((), ())), preferred_element_type=F32)
    return scores, jnp.max(scores, axis=1, keepdims=True)


def queries_of(q_ref, n):
    return jnp.concatenate([q_ref[slot(n, 0), 0:64], q_ref[slot(n, 1), 0:64]], axis=0)


def first_half_kernel(q_ref, sum_out, top_out):
    keys, vals = halves(q_ref, 64)
    for n in range(8):
        rows = slice(128 * n, 128 * n + 128)
        scores, top = scores_of(queries_of(q_ref, n), keys)
        weights = jnp.exp2((scores - top) * SCALE).astype(BF)
        sum_out[rows] = jnp.dot(weights, vals, preferred_element_type=F32)
        top_out[rows] = jnp.broadcast_to(top, (128, HD))


def second_half_kernel(q_ref, kv_ref, sum_ref, top_ref, out_ref, windows):
    keys, vals = halves(kv_ref, 0)
    edge = jnp.zeros((16, HD), F32)
    for s in range(2):
        windows[slot(0, s), 0:16] = edge
        windows[slot(7, s), 80:96] = edge
    for n in range(8):
        rows = slice(128 * n, 128 * n + 128)
        scores, top = scores_of(queries_of(q_ref, n), keys)
        before = top_ref[rows, 0:1]
        top = jnp.maximum(top, before)
        weights = jnp.exp2((scores - top) * SCALE).astype(BF)
        kept = jnp.exp2((before - top) * SCALE)
        both = sum_ref[rows] * kept + jnp.dot(weights, vals, preferred_element_type=F32)
        done = both[:, 0:HD] / both[:, HD : 2 * HD]
        for s in range(2):
            half = done[64 * s : 64 * s + 64]
            windows[slot(n, s), 16:80] = half
            if n < 7:
                windows[slot(n + 1, s), 0:16] = half[48:64]
            if n > 0:
                windows[slot(n - 1, s), 80:96] = half[0:16]
    row = lax.broadcasted_iota(jnp.int32, (32, 96), 0)
    col = lax.broadcasted_iota(jnp.int32, (32, 96), 1)
    for s in range(2):
        pick = (col == (row // 2) * 8 + row % 2 + 6 * s).astype(F32).astype(BF)
        for n in range(8):
            near = jnp.dot(pick, windows[slot(n, 1 - s)].astype(BF), preferred_element_type=F32)
            out_ref[slot(n, s)] = jnp.concatenate([windows[slot(n, s)], near[0:24]], axis=0).astype(BF)


def project_kernel(a_ref, w_ref, out_ref):
    for x in range(2):
        rows = jnp.concatenate([a_ref[slot(h, x)] for h in range(H)], axis=1)
        projected = jnp.dot(rows, w_ref[...], preferred_element_type=F32)
        scale = lax.rsqrt(jnp.mean(projected * projected, axis=1, keepdims=True) + 1e-06)
        out_ref[x] = (projected * scale).astype(BF)


def laid_out(normed):
    seq = lax.axis_index("seq")
    row = lax.broadcasted_iota(jnp.int32, (12, 8, 256), 1)
    slabs = []
    for x in range(2):
        rows = normed[x].astype(F32)
        middle = pltpu.roll(rows[0:96].reshape(12, 8, 256), 2, 1)
        near = rows[96:120].reshape(3, 8, 256)
        ends = [pltpu.roll(near, 8 - 2 * k, 1) if k else near for k in range(4)]
        ends = jnp.stack(ends, axis=1).reshape(12, 8, 256)
        upper = jnp.where(row < 2, jnp.where(seq == 1, ends, 0.0), middle)
        lower = jnp.where((row < 4) & (seq == 0), pltpu.roll(ends, 2, 1), 0.0)
        lower = jnp.where(row < 2, middle, lower)
        slabs.append(jnp.concatenate([upper, lower], axis=1).reshape(192, 256).astype(BF))
    return slabs


def merge_kernel(w_ref, out_ref):
    def both(parts):
        return ((parts[0], parts[1] + parts[2]), (parts[0] + parts[1], parts[2]))

    taps = [[[w_ref[9 * a + 3 * b + c].astype(F32) for c in range(3)] for b in range(3)] for a in range(3)]
    on_z = [[[m for p in both(taps[a][b]) for m in p] for b in range(3)] for a in range(3)]
    for n in range(4):
        on_y = [both([on_z[a][b][n] for b in range(3)]) for a in range(3)]
        for py in range(2):
            for b in range(2):
                on_x = both([on_y[a][py][b] for a in range(3)])
                for px in range(2):
                    for a in range(2):
                        rows = (2 * a + b) * 128
                        out_ref[2 * px + py, rows : rows + 128, n * 128 : (n + 1) * 128] = on_x[px][a].astype(BF)


def shifted(x, by):
    return pltpu.roll(x, by % x.shape[0], 0)


def x_tile():
    return 2 * lax.axis_index("z") + lax.axis_index("core")


def taps(w1_ref, a, b):
    t = 9 * a + 3 * b
    return jnp.concatenate([w1_ref[t], w1_ref[t + 1], w1_ref[t + 2]], axis=1)


def own_conv_kernel(own_ref, w1_ref, out_ref):
    slabs = laid_out(own_ref[...])
    for x in range(4):
        total = jnp.zeros((160, 384), F32)
        for a in range(3):
            if 2 <= x + a < 4:
                for b in range(3):
                    part = slabs[x + a - 2][16 * b : 16 * b + 160]
                    total = total + jnp.dot(part, taps(w1_ref, a, b), preferred_element_type=F32)
        out_ref[x] = total


def side(at_left, slabs, own_ref, w1_ref):
    gx, gy, seq = x_tile(), 2 * lax.axis_index("chip_x") + lax.axis_index("low_y"), lax.axis_index("seq")
    row = lax.broadcasted_iota(jnp.int32, (160, 128), 0)
    at_z = seq * 8 - 1 + row % 16
    at_y = gy * 8 - 1 + row // 16
    inside = (at_y >= 0) & (at_y < 64) & (at_z >= 0) & (at_z < 16)
    first_tap = jnp.where(at_left, 0, 1)
    outer = [(slabs[0], first_tap), (slabs[1], first_tap + 1)]
    inner = [(jnp.where(at_left, slabs[1], slabs[0]), jnp.where(at_left, 0, 2))]
    results = []
    for x, terms in ((jnp.where(at_left, 0, 3), outer), (jnp.where(at_left, 1, 2), inner)):
        total = own_ref[x]
        for slab, a in terms:
            for b in range(3):
                total = total + jnp.dot(slab[16 * b : 16 * b + 160], taps(w1_ref, a, b), preferred_element_type=F32)
        first = total[:, 0:128] + shifted(total[:, 128:256], -1) + shifted(total[:, 256:384], -2)
        value = first / (1.0 + jnp.exp(-first))
        at_x = gx * 2 - 1 + x
        results.append((x, jnp.where(inside & (at_x >= 0) & (at_x < 32), value, 0.0).astype(BF)))
    return results


def near_conv_kernel(near_ref, own_ref, w1_ref, out_ref):
    at_left = lax.axis_index("core") == 1
    slabs = laid_out(near_ref[1 - lax.axis_index("core")])
    for n, (_, rows) in enumerate(side(at_left, slabs, own_ref, w1_ref)):
        out_ref[n] = rows


def conv_kernel(own_ref, done_ref, far_ref, w1_ref, w2_ref, out_hbm, hidden, field, ready, sems):
    gx = x_tile()
    at_left = lax.axis_index("core") == 0
    there = jnp.where(at_left, gx > 0, gx < 15)
    slabs = [jnp.where(there, slab, jnp.zeros_like(slab)) for slab in laid_out(far_ref[...])]
    hidden[jnp.where(at_left, 3, 0)] = done_ref[0]
    hidden[jnp.where(at_left, 2, 1)] = done_ref[1]
    for x, rows in side(at_left, slabs, own_ref, w1_ref):
        hidden[x] = rows
    copies = []
    for px in range(2):
        for py in range(2):
            rows = [
                [hidden[i + px + a, 16 * (py + b) : 16 * (py + b) + 128] for a in range(2) for b in range(2)]
                for i in range(2)
            ]
            rows = jnp.concatenate([jnp.concatenate(parts, axis=1) for parts in rows], axis=0)
            parts = jnp.dot(rows, w2_ref[2 * px + py], preferred_element_type=F32)
            even = parts[:, 0:128] + shifted(parts[:, 128:256], -1)
            odd = shifted(parts[:, 256:384], -1) + shifted(parts[:, 384:512], -2)
            for pz, part in ((0, even), (1, odd)):
                part = part.reshape(2, 8, 16, 128)
                for i in range(2):
                    for j in range(8):
                        field[2 * i + px, 2 * j + py, pl.ds(pz, 8, stride=2), :] = part[i, j, 0:8]
        for x in (px, px + 2):
            ready[x] = field[x].astype(BF)
            copies.append(pltpu.make_async_copy(ready.at[x], out_hbm.at[x], sems.at[x]))
            copies[-1].start()
    for copy in copies:
        copy.wait()


def body(queries, keys, values, w_out, conv_first, conv_second):
    rows = queries.reshape(2, 64, H * HD)
    in_hbm = [pltpu.with_memory_space_constraint(array, pltpu.HBM) for array in (rows, keys, values)]
    scratch = [pltpu.VMEM((8, H * HD), BF), pltpu.VMEM((8, H * HD), BF), pltpu.SemaphoreType.DMA((3,))]
    spread, rows = call(spread_kernel, [(8, 16, H * HD), rows.shape], [BF, BF], [HB] * 3, scratch)(*in_hbm)
    tokens = lax.all_to_all(spread, "z", 0, 0, tiled=True)
    sent = call(pack_kernel, [(16, 192, HD)], [BF], [VM] * 2)(rows, tokens)
    got = lax.all_to_all(sent, ("seq", "low_y", "chip_x"), 0, 0, tiled=True)
    other = lax.ppermute(got[:, 64:192], "core", [(0, 1), (1, 0)])
    summed, top = call(first_half_kernel, [(1024, 2 * HD), (1024, HD)], [F32, F32], [VM])(got)
    attended = call(second_half_kernel, [(16, 120, HD)], [BF], [VM] * 4, [pltpu.VMEM((16, 96, HD), F32)])(got, other, summed, top)
    back = lax.all_to_all(attended, ("seq", "low_y", "chip_x"), 0, 0, tiled=True)
    normed = call(project_kernel, [(2, 120, 256)], [BF], [VM, VM])(back, w_out)
    far = lax.ppermute(normed, ("z", "core"), [(i, (i - 1 + 2 * (i % 2)) % 16) for i in range(16)])
    near = lax.all_gather(normed, "core")
    w1 = conv_first.reshape(27, 256, 128)
    merged = call(merge_kernel, [(4, 512, 512)], [BF], [VM])(conv_second.reshape(27, 128, 128))
    own_part = call(own_conv_kernel, [(4, 160, 384)], [F32], [VM, VM])(normed, w1)
    done = call(near_conv_kernel, [(2, 160, 128)], [BF], [VM] * 3)(near, own_part, w1)
    scratch = [
        pltpu.VMEM((4, 160, 128), BF),
        pltpu.VMEM((4, 16, 16, 128), F32),
        pltpu.VMEM((4, 16, 16, 128), BF),
        pltpu.SemaphoreType.DMA((4,)),
    ]
    final = call(conv_kernel, [(4, 16, 16, 128)], [BF], [VM] * 5, scratch, HB)
    return final(own_part, done, far, w1, merged)


def solution(mesh):
    cut = Mesh(mesh.devices.reshape(8, 2, 4, 2, 2), ("z", "core", "chip_x", "low_y", "seq"))
    tokens = P(("z", "core", "chip_x", "low_y", "seq"), None)
    voxels = P(("z", "core"), ("chip_x", "low_y"), "seq", None)
    return jax.shard_map(
        body, mesh=cut, in_specs=(voxels, tokens, tokens, P(), P(), P()), out_specs=voxels, check_vma=False
    )
```

```python
import jax
import jax.numpy as jnp
from jax import lax
from jax.experimental import pallas as pl
from jax.experimental.pallas import tpu as pltpu
from jax.sharding import Mesh, PartitionSpec as P

H = 8
HD = 128
BF = jnp.bfloat16
F32 = jnp.float32
VM = pl.BlockSpec(memory_space=pltpu.VMEM)
HB = pl.BlockSpec(memory_space=pltpu.HBM)
SCALE = HD**-0.5 * 1.4426950408889634


def call(kernel, shapes, dtypes, in_specs, scratch=(), out_spec=VM):
    outs = [jax.ShapeDtypeStruct(shape, dtype) for shape, dtype in zip(shapes, dtypes)]
    one = len(outs) == 1
    return pl.pallas_call(
        kernel,
        out_shape=outs[0] if one else outs,
        in_specs=in_specs,
        out_specs=out_spec if one else [VM] * len(outs),
        scratch_shapes=list(scratch),
        compiler_params=pltpu.CompilerParams(vmem_limit_bytes=24 * 1024 * 1024),
        cost_estimate=pl.CostEstimate(flops=10**6, bytes_accessed=10000, transcendentals=0),
    )


def slot(tile, half):
    return 8 * half + 4 * (tile % 2) + tile // 2


def spread_kernel(q_hbm, k_hbm, v_hbm, out_ref, q_ref, k_ref, v_ref, sems):
    copies = [
        pltpu.make_async_copy(src, dst, sems.at[i])
        for i, (src, dst) in enumerate(((k_hbm, k_ref), (v_hbm, v_ref), (q_hbm, q_ref)))
    ]
    for copy in copies:
        copy.start()
    for copy in copies[0:2]:
        copy.wait()
    pair = jnp.concatenate([k_ref[...].astype(F32), v_ref[...].astype(F32)], axis=0).astype(BF)
    for z in range(8):
        out_ref[z] = pair
    copies[2].wait()


def pack_kernel(q_ref, kv_ref, out_ref):
    for h in range(H):
        cols = slice(h * HD, (h + 1) * HD)
        pairs = [kv_ref[z, :, cols].astype(F32) for z in range(8)]
        keys = jnp.concatenate([pair[0:8] for pair in pairs], axis=0).astype(BF)
        vals = jnp.concatenate([pair[8:16] for pair in pairs], axis=0).astype(BF)
        for s in range(2):
            out_ref[slot(h, s), 0:64] = q_ref[s, :, cols]
            out_ref[slot(h, s), 64:128] = keys
            out_ref[slot(h, s), 128:192] = vals


def halves(ref, at):
    keys = ref[:, at : at + 64].reshape(1024, HD)
    return keys, jnp.concatenate([ref[:, at + 64 : at + 128].reshape(1024, HD), jnp.ones((1024, HD), BF)], axis=1)


def scores_of(q, keys):
    scores = lax.dot_general(q, keys, (((1,), (1,)), ((), ())), preferred_element_type=F32)
    return scores, jnp.max(scores, axis=1, keepdims=True)


def queries_of(q_ref, n):
    return jnp.concatenate([q_ref[slot(n, 0), 0:64], q_ref[slot(n, 1), 0:64]], axis=0)


def first_half_kernel(q_ref, sum_out, top_out):
    keys, vals = halves(q_ref, 64)
    for n in range(8):
        rows = slice(128 * n, 128 * n + 128)
        scores, top = scores_of(queries_of(q_ref, n), keys)
        weights = jnp.exp2((scores - top) * SCALE).astype(BF)
        sum_out[rows] = jnp.dot(weights, vals, preferred_element_type=F32)
        top_out[rows] = jnp.broadcast_to(top, (128, HD))


def second_half_kernel(q_ref, kv_ref, sum_ref, top_ref, out_ref, windows):
    keys, vals = halves(kv_ref, 0)
    edge = jnp.zeros((16, HD), F32)
    for s in range(2):
        windows[slot(0, s), 0:16] = edge
        windows[slot(7, s), 80:96] = edge
    for n in range(8):
        rows = slice(128 * n, 128 * n + 128)
        scores, top = scores_of(queries_of(q_ref, n), keys)
        before = top_ref[rows, 0:1]
        top = jnp.maximum(top, before)
        weights = jnp.exp2((scores - top) * SCALE).astype(BF)
        kept = jnp.exp2((before - top) * SCALE)
        both = sum_ref[rows] * kept + jnp.dot(weights, vals, preferred_element_type=F32)
        done = both[:, 0:HD] / both[:, HD : 2 * HD]
        for s in range(2):
            half = done[64 * s : 64 * s + 64]
            windows[slot(n, s), 16:80] = half
            if n < 7:
                windows[slot(n + 1, s), 0:16] = half[48:64]
            if n > 0:
                windows[slot(n - 1, s), 80:96] = half[0:16]
    row = lax.broadcasted_iota(jnp.int32, (32, 96), 0)
    col = lax.broadcasted_iota(jnp.int32, (32, 96), 1)
    for s in range(2):
        pick = (col == (row // 2) * 8 + row % 2 + 6 * s).astype(F32).astype(BF)
        for n in range(0, 8, 2):
            two = jnp.concatenate([windows[slot(n, 1 - s)], windows[slot(n + 1, 1 - s)]], axis=1).astype(BF)
            near = jnp.dot(pick, two, preferred_element_type=F32)
            for m, part in ((n, near[0:24, 0:HD]), (n + 1, near[0:24, HD : 2 * HD])):
                out_ref[slot(m, s)] = jnp.concatenate([windows[slot(m, s)], part], axis=0).astype(BF)


def project_kernel(a_ref, w_ref, out_ref):
    for x in range(2):
        rows = jnp.concatenate([a_ref[slot(h, x)] for h in range(H)], axis=1)
        projected = jnp.dot(rows, w_ref[...], preferred_element_type=F32)
        scale = lax.rsqrt(jnp.mean(projected * projected, axis=1, keepdims=True) + 1e-06)
        out_ref[x] = (projected * scale).astype(BF)


def laid_out(normed):
    seq = lax.axis_index("seq")
    row = lax.broadcasted_iota(jnp.int32, (12, 8, 256), 1)
    slabs = []
    for x in range(2):
        rows = normed[x].astype(F32)
        middle = pltpu.roll(rows[0:96].reshape(12, 8, 256), 2, 1)
        near = rows[96:120].reshape(3, 8, 256)
        ends = [pltpu.roll(near, 8 - 2 * k, 1) if k else near for k in range(4)]
        ends = jnp.stack(ends, axis=1).reshape(12, 8, 256)
        upper = jnp.where(row < 2, jnp.where(seq == 1, ends, 0.0), middle)
        lower = jnp.where((row < 4) & (seq == 0), pltpu.roll(ends, 2, 1), 0.0)
        lower = jnp.where(row < 2, middle, lower)
        slabs.append(jnp.concatenate([upper, lower], axis=1).reshape(192, 256).astype(BF))
    return slabs


def merge_kernel(w_ref, out_ref):
    def both(parts):
        return ((parts[0], parts[1] + parts[2]), (parts[0] + parts[1], parts[2]))

    taps = [[[w_ref[9 * a + 3 * b + c].astype(F32) for c in range(3)] for b in range(3)] for a in range(3)]
    on_z = [[[m for p in both(taps[a][b]) for m in p] for b in range(3)] for a in range(3)]
    for n in range(4):
        on_y = [both([on_z[a][b][n] for b in range(3)]) for a in range(3)]
        for py in range(2):
            for b in range(2):
                on_x = both([on_y[a][py][b] for a in range(3)])
                for px in range(2):
                    for a in range(2):
                        rows = (2 * a + b) * 128
                        out_ref[2 * px + py, rows : rows + 128, n * 128 : (n + 1) * 128] = on_x[px][a].astype(BF)


def shifted(x, by):
    return pltpu.roll(x, by % x.shape[0], 0)


def x_tile():
    return 2 * lax.axis_index("z") + lax.axis_index("core")


def taps(w1_ref, a, b):
    t = 9 * a + 3 * b
    return jnp.concatenate([w1_ref[t], w1_ref[t + 1], w1_ref[t + 2]], axis=1)


def own_conv_kernel(own_ref, w1_ref, out_ref):
    slabs = laid_out(own_ref[...])
    for x in range(4):
        total = jnp.zeros((160, 384), F32)
        for a in range(3):
            if 2 <= x + a < 4:
                for b in range(3):
                    part = slabs[x + a - 2][16 * b : 16 * b + 160]
                    total = total + jnp.dot(part, taps(w1_ref, a, b), preferred_element_type=F32)
        out_ref[x] = total


def side(at_left, slabs, own_ref, w1_ref):
    gx, gy, seq = x_tile(), 2 * lax.axis_index("chip_x") + lax.axis_index("low_y"), lax.axis_index("seq")
    row = lax.broadcasted_iota(jnp.int32, (160, 128), 0)
    at_z = seq * 8 - 1 + row % 16
    at_y = gy * 8 - 1 + row // 16
    inside = (at_y >= 0) & (at_y < 64) & (at_z >= 0) & (at_z < 16)
    first_tap = jnp.where(at_left, 0, 1)
    outer = [(slabs[0], first_tap), (slabs[1], first_tap + 1)]
    inner = [(jnp.where(at_left, slabs[1], slabs[0]), jnp.where(at_left, 0, 2))]
    results = []
    for x, terms in ((jnp.where(at_left, 0, 3), outer), (jnp.where(at_left, 1, 2), inner)):
        total = own_ref[x]
        for slab, a in terms:
            for b in range(3):
                total = total + jnp.dot(slab[16 * b : 16 * b + 160], taps(w1_ref, a, b), preferred_element_type=F32)
        first = total[:, 0:128] + shifted(total[:, 128:256], -1) + shifted(total[:, 256:384], -2)
        value = first / (1.0 + jnp.exp(-first))
        at_x = gx * 2 - 1 + x
        results.append((x, jnp.where(inside & (at_x >= 0) & (at_x < 32), value, 0.0).astype(BF)))
    return results


def near_conv_kernel(near_ref, own_ref, w1_ref, out_ref):
    at_left = lax.axis_index("core") == 1
    slabs = laid_out(near_ref[1 - lax.axis_index("core")])
    for n, (_, rows) in enumerate(side(at_left, slabs, own_ref, w1_ref)):
        out_ref[n] = rows


def conv_kernel(own_ref, done_ref, far_ref, w1_ref, w2_ref, out_hbm, hidden, field, ready, sems):
    gx = x_tile()
    at_left = lax.axis_index("core") == 0
    there = jnp.where(at_left, gx > 0, gx < 15)
    slabs = [jnp.where(there, slab, jnp.zeros_like(slab)) for slab in laid_out(far_ref[...])]
    hidden[jnp.where(at_left, 3, 0)] = done_ref[0]
    hidden[jnp.where(at_left, 2, 1)] = done_ref[1]
    for x, rows in side(at_left, slabs, own_ref, w1_ref):
        hidden[x] = rows
    copies = []
    for px in range(2):
        for py in range(2):
            rows = [
                [hidden[i + px + a, 16 * (py + b) : 16 * (py + b) + 128] for a in range(2) for b in range(2)]
                for i in range(2)
            ]
            rows = jnp.concatenate([jnp.concatenate(parts, axis=1) for parts in rows], axis=0)
            parts = jnp.dot(rows, w2_ref[2 * px + py], preferred_element_type=F32)
            even = parts[:, 0:128] + shifted(parts[:, 128:256], -1)
            odd = shifted(parts[:, 256:384], -1) + shifted(parts[:, 384:512], -2)
            for pz, part in ((0, even), (1, odd)):
                part = part.reshape(2, 8, 16, 128)
                for i in range(2):
                    for j in range(8):
                        field[2 * i + px, 2 * j + py, pl.ds(pz, 8, stride=2), :] = part[i, j, 0:8]
        for x in (px, px + 2):
            ready[x] = field[x].astype(BF)
            copies.append(pltpu.make_async_copy(ready.at[x], out_hbm.at[x], sems.at[x]))
            copies[-1].start()
    for copy in copies:
        copy.wait()


def body(queries, keys, values, w_out, conv_first, conv_second):
    rows = queries.reshape(2, 64, H * HD)
    in_hbm = [pltpu.with_memory_space_constraint(array, pltpu.HBM) for array in (rows, keys, values)]
    scratch = [pltpu.VMEM((8, H * HD), BF), pltpu.VMEM((8, H * HD), BF), pltpu.SemaphoreType.DMA((3,))]
    spread, rows = call(spread_kernel, [(8, 16, H * HD), rows.shape], [BF, BF], [HB] * 3, scratch)(*in_hbm)
    tokens = lax.all_to_all(spread, "z", 0, 0, tiled=True)
    sent = call(pack_kernel, [(16, 192, HD)], [BF], [VM] * 2)(rows, tokens)
    got = lax.all_to_all(sent, ("seq", "low_y", "chip_x"), 0, 0, tiled=True)
    other = lax.ppermute(got[:, 64:192], "core", [(0, 1), (1, 0)])
    summed, top = call(first_half_kernel, [(1024, 2 * HD), (1024, HD)], [F32, F32], [VM])(got)
    attended = call(second_half_kernel, [(16, 120, HD)], [BF], [VM] * 4, [pltpu.VMEM((16, 96, HD), F32)])(got, other, summed, top)
    back = lax.all_to_all(attended, ("seq", "low_y", "chip_x"), 0, 0, tiled=True)
    normed = call(project_kernel, [(2, 120, 256)], [BF], [VM, VM])(back, w_out)
    far = lax.ppermute(normed, ("z", "core"), [(i, (i - 1 + 2 * (i % 2)) % 16) for i in range(16)])
    near = lax.all_gather(normed, "core")
    w1 = conv_first.reshape(27, 256, 128)
    merged = call(merge_kernel, [(4, 512, 512)], [BF], [VM])(conv_second.reshape(27, 128, 128))
    own_part = call(own_conv_kernel, [(4, 160, 384)], [F32], [VM, VM])(normed, w1)
    done = call(near_conv_kernel, [(2, 160, 128)], [BF], [VM] * 3)(near, own_part, w1)
    scratch = [
        pltpu.VMEM((4, 160, 128), BF),
        pltpu.VMEM((4, 16, 16, 128), F32),
        pltpu.VMEM((4, 16, 16, 128), BF),
        pltpu.SemaphoreType.DMA((4,)),
    ]
    final = call(conv_kernel, [(4, 16, 16, 128)], [BF], [VM] * 5, scratch, HB)
    return final(own_part, done, far, w1, merged)


def solution(mesh):
    cut = Mesh(mesh.devices.reshape(8, 2, 4, 2, 2), ("z", "core", "chip_x", "low_y", "seq"))
    tokens = P(("z", "core", "chip_x", "low_y", "seq"), None)
    voxels = P(("z", "core"), ("chip_x", "low_y"), "seq", None)
    return jax.shard_map(
        body, mesh=cut, in_specs=(voxels, tokens, tokens, P(), P(), P()), out_specs=voxels, check_vma=False
    )
```
